256 devices in a mesh: dp: 16 (over x_lo, y, core), shard: 16 (over x_hi, z).
Axes of the slice: x: 4 (x_hi: 2, x_lo: 2; x = x_hi * 2 + x_lo), y: 4, z: 8, core: 2. Of those that a mesh axis runs over, the one named last changes fastest.
Arguments:
- inputs: bfloat16 [32768, 8192], P(('dp', 'shard')), may hold values from -6 to 6
- cotangent: bfloat16 [32768, 1024], P(('dp', 'shard')), may hold values from -160 to 160
- weight: bfloat16 [8192, 1024], P('shard'), may hold values from -0.0625 to 0.0625
- projector: bfloat16 [8192, 1024], P('shard'), may hold values from -0.0625 to 0.0625
- first_moment_state: float32 [1024, 1024], P(('dp', 'shard')), may hold values from -6 to 6
- second_moment_state: float32 [1024, 1024], P(('dp', 'shard')), may hold values from 0.25 to 4
Outputs:
- input_gradient: bfloat16 [32768, 8192], P(('dp', 'shard'))
- weight_update: bfloat16 [8192, 1024], P('shard')
- new_first: float32 [1024, 1024], P(('dp', 'shard'))
- new_second: float32 [1024, 1024], P(('dp', 'shard'))
The draws below stay inside these ranges and needn't reach their ends.
All inputs are finite; a program needn't handle non-finite values.
Results may differ from the reference program's by a relative error of at most 0.009.
Values may be sent and summed in bfloat16 or wider, within the bound.
A program may use at most 128 MiB of HBM per device.

```python
import math
import jax
import jax.numpy as jnp
from jax import lax

MODEL_WIDTH = 8192
KEY_OUTPUTS = 1024
PROJECTION_RANK = 1024
TOK_DEV = 128
TOKEN_COUNT = 32768
N_DP = 16
N_SHARD = 16


def draw_cotangent(key, part):
    key = jax.random.fold_in(key, 11)
    first_random_key = jax.random.fold_in(key, 0)
    third_random_key = jax.random.fold_in(key, 2)
    column_index = jnp.arange(KEY_OUTPUTS, dtype=jnp.float32) / (KEY_OUTPUTS - 1)
    value_entries = jnp.clip(jax.random.normal(first_random_key, (TOKEN_COUNT, KEY_OUTPUTS), jnp.float32), -4.0, 4.0)
    value_entries = value_entries * (1.0 + 2.0 * column_index)[None, :]
    device_count = N_DP * N_SHARD
    block_width = KEY_OUTPUTS // device_count
    token_owner = (jnp.arange(TOKEN_COUNT, dtype=jnp.int32) // TOK_DEV)[:, None]
    column_owner = (jnp.arange(KEY_OUTPUTS, dtype=jnp.int32) // block_width)[None, :]
    pairing = jax.random.permutation(third_random_key, device_count).astype(jnp.int32)
    opposite = (token_owner + device_count // 2) % device_count
    paired = pairing[token_owner[:, 0]][:, None]
    heavy = jnp.logical_or(column_owner == opposite, column_owner == paired)
    value_entries = value_entries * jnp.where(heavy, 8.0, 1.0)
    return value_entries.astype(jnp.bfloat16)


def shard_levels(key, dims, cuts, least, high):
    loudness, own = 1.0, jax.random.fold_in(key, 6)
    for dim, blocks in cuts:
        heights = jnp.exp(jax.random.uniform(jax.random.fold_in(own, dim), (blocks,), jnp.float32, least / len(cuts), high / len(cuts)))
        loudness = loudness * jnp.repeat(heights, dims[dim] // blocks).reshape([-1 if axis == dim else 1 for axis in range(len(dims))])
    return loudness


def centred(stream_key, dims, spread, most, cuts=(), held_as=jnp.bfloat16):
    entries = jax.random.normal(stream_key, dims, jnp.float32) * spread
    if len(cuts) > 0:
        entries = shard_levels(stream_key, dims, cuts, -0.22, 0.18) * entries
    return jnp.clip(entries, min=-most, max=most).astype(held_as)


def setup_inputs(seed: int = 0) -> dict:
    key_list = jax.random.split(jax.random.key(seed), 7)
    inputs = centred(key_list[0], (TOKEN_COUNT, MODEL_WIDTH), 1.0, 6.0, ((0, 256),))
    cotangent = draw_cotangent(jax.random.fold_in(key_list[6], 71), 0)
    weight = centred(key_list[2], (MODEL_WIDTH, KEY_OUTPUTS), MODEL_WIDTH ** -0.5, 0.0625, ((0, 16),))
    projector = centred(key_list[3], (MODEL_WIDTH, PROJECTION_RANK), MODEL_WIDTH ** -0.5, 0.0625, ((0, 16),))
    first_moment_state = centred(key_list[4], (KEY_OUTPUTS, PROJECTION_RANK), 1.0, 6.0, ((0, 256),), jnp.float32)
    second_moment_state = jnp.clip(jnp.exp(math.log(4.0) - 2.7725887 * jax.random.uniform(key_list[5], (KEY_OUTPUTS, PROJECTION_RANK), jnp.float32) ** shard_levels(key_list[5], (KEY_OUTPUTS, PROJECTION_RANK), ((0, 256),), -0.2, 0.2)), 0.25, 4.0)
    return {"inputs": inputs, "cotangent": cotangent, "weight": weight, "projector": projector, "first_moment_state": first_moment_state, "second_moment_state": second_moment_state}


beta_one = 0.9
beta_two = 0.999
bias_one = 1.0
bias_two = 0.632304575

def reference(inputs, cotangent, weight, projector, first_moment_state, second_moment_state):
    input_gradient = lax.dot_general(cotangent, weight, (((1,), (1,)), ((), ())), preferred_element_type=jnp.float32).astype(jnp.bfloat16)
    shard_width = MODEL_WIDTH // N_SHARD
    projected = jnp.zeros((inputs.shape[0], PROJECTION_RANK), jnp.float32)
    for position in range(N_SHARD):
        part_term = jnp.dot(inputs[:, position * shard_width:(position + 1) * shard_width], projector[position * shard_width:(position + 1) * shard_width], preferred_element_type=jnp.float32)
        projected = projected + lax.optimization_barrier(part_term.astype(jnp.bfloat16)).astype(jnp.float32)
    key_gradient = lax.dot_general(cotangent.astype(jnp.float32), projected, (((0,), (0,)), ((), ())), precision=lax.Precision.HIGHEST, preferred_element_type=jnp.float32)
    mean_squared_value = jnp.sum(key_gradient * key_gradient) / (KEY_OUTPUTS * PROJECTION_RANK)
    step_factor = jnp.minimum(1.0, lax.rsqrt(mean_squared_value + 1e-06))
    clipped = key_gradient * step_factor
    new_first = beta_one * first_moment_state + (1.0 - beta_one) * clipped
    new_second = beta_two * second_moment_state + (1.0 - beta_two) * clipped * clipped
    direction = (new_first / bias_one / (jnp.sqrt(new_second / bias_two) + 1e-08)).astype(jnp.bfloat16)
    weight_update = lax.dot_general(projector, direction, (((1,), (1,)), ((), ())), preferred_element_type=jnp.float32).astype(jnp.bfloat16)
    return (input_gradient, weight_update, new_first, new_second)
```

```python
import jax
import jax.numpy as jnp
from jax import lax
from jax.experimental import pallas as pl
from jax.experimental.pallas import tpu as pltpu
from jax.sharding import PartitionSpec as P

MESH = pl.DeviceIdType.MESH
F32 = jnp.float32
BF16 = jnp.bfloat16

TOKENS = 128
WIDTH = 8192
OUTS = 1024
RANK = 1024
ENTRIES = OUTS * RANK

beta_one = 0.9
beta_two = 0.999
bias_one = 1.0
bias_two = 0.632304575

NN = (((1,), (0,)), ((), ()))
NT = (((1,), (1,)), ((), ()))


def dot(a, b, dims=NN):
    return lax.dot_general(a, b, dims, preferred_element_type=F32)


def flip(bit, by):
    return 1 - bit if by else bit


def wait_bytes(ref, sem):
    pltpu.make_async_copy(ref, ref, sem).wait()


PAIRS = ((0, 0), (0, 1), (1, 0), (1, 1))
ORDER = (1, 3, 2)


def kernel(
    inp, cot, w, p, m_in, v_in,
    ig, wu, nf, nv,
    cx, cy, ct, xx, pg, wg, pblk, mf, mb, igb,
    s0, r0, a_keep, a0, a1, ra0, ra1, b0, b1, rb0, rb1, cs, rc, gz, mvz, ss, sr_a, sr_b, df, dall,
    local_sem, c_send, c_recv, x_send, x_recv, pre_send, pre_recv,
    ring_send_sem, ring_recv_sem, mv_send, mv_recv, o_send, o_recv,
    s_send, s_recv, a_send, a_recv, b_send, b_recv, z_send, z_recv, g_send, g_recv,
    q_send, q_recv, d_send, d_recv, e_send, e_recv,
):
    d = lax.axis_index("dp")
    s = lax.axis_index("shard")
    xl = d // 8
    y = (d // 2) % 4
    yh = y // 2
    yl = y % 2
    c = d % 2
    h = s // 8
    z = s % 8

    def device(xl_, yh_, yl_, c_, h_, z_):
        return ((xl_ * 4 + yh_ * 2 + yl_) * 2 + c_, h_ * 8 + z_)

    def partner(axis, i, kc):
        hi, lo = PAIRS[i]
        if axis == 0:
            return device(flip(xl, lo), yh, yl, flip(c, kc), flip(h, hi), z)
        return device(xl, flip(yh, hi), flip(yl, lo), flip(c, kc), h, z)

    def z_peer(k):
        return device(xl, yh, yl, c, h, (z + k) % 8)

    sends = []

    def send(src, dst, ss_, rs_, to):
        copy = pltpu.make_async_remote_copy(
            src_ref=src, dst_ref=dst, send_sem=ss_, recv_sem=rs_, device_id=to, device_id_type=MESH
        )
        copy.start()
        sends.append(copy)

    own_c = pltpu.make_async_copy(cot, cx.at[0], local_sem.at[0])
    own_c.start()
    own_p = pltpu.make_async_copy(p, pblk, local_sem.at[1])
    own_p.start()

    barrier = pltpu.get_barrier_semaphore()
    peers = [partner(0, i, kc) for i in range(4) for kc in range(2) if (i, kc) != (0, 0)]
    peers += [partner(1, i, kc) for i in range(1, 4) for kc in range(2)]
    peers += [z_peer(k) for k in range(1, 8)]
    for peer in peers:
        pl.semaphore_signal(barrier, inc=1, device_id=peer, device_id_type=MESH)

    odd = z % 2
    quarter = (1 - odd) * (xl * 2 + c) + odd * (yl * 2 + c)
    rows = pl.ds(pl.multiple_of(quarter * 128, 128), 128)
    foreign = odd * (h + yh - 2 * h * yh)

    def slot_of(zz):
        return (zz % 2) * 4 + zz // 2

    slot = slot_of(z)

    @pl.when(foreign == 0)
    def _():
        for n, (src, dst) in enumerate(((p, pg), (w, wg))):
            pltpu.make_async_copy(src.at[rows], dst.at[slot], local_sem.at[2 + n]).start()


    def columns(axis, i, kc, t):
        hi, lo = PAIRS[i]
        if axis == 0:
            q = flip(xl, lo) * 2 + flip(c, kc)
            block = flip(h, hi) * 8 + 2 * t
        else:
            q = flip(yl, lo) * 2 + flip(c, kc)
            block = flip(yh, hi) * 8 + 2 * t + 1
        return pl.ds(pl.multiple_of(block * 512 + q * 128, 128), 128)

    for axis in range(2):
        for t in range(4):
            pltpu.make_async_copy(
                inp.at[:, columns(axis, 0, 0, t)],
                xx.at[axis, 0, :, pl.ds(t * 128, 128)],
                local_sem.at[4 + axis],
            ).start()

    for n, ref in enumerate((m_in, v_in)):
        for half in range(2):
            mvz[z, n, half * 4 : half * 4 + 4, :] = ref[:, half * 512 : half * 512 + 512]

    pl.semaphore_wait(barrier, len(peers))

    own_c.wait()
    for axis in range(2):
        for i in ORDER:
            dst = (cx if axis == 0 else cy).at[2 * i]
            send(cx.at[0], dst, c_send.at[axis, i], c_recv.at[axis, i, 0], partner(axis, i, 0))
    send(cx.at[0], cx.at[1], c_send.at[0, 0], c_recv.at[0, 0, 1], partner(0, 0, 1))

    @pl.when(odd * (1 - foreign) == 1)
    def _():
        for n, (src, dst) in enumerate(((p, pg), (w, wg))):
            pltpu.make_async_remote_copy(
                src_ref=src.at[rows], dst_ref=dst.at[slot], send_sem=pre_send.at[n], recv_sem=pre_recv.at[n],
                device_id=partner(0, 3, 0), device_id_type=MESH,
            ).start()

    rings = (pg, wg)

    def ring_send(n, direction, t, a):
        sign = 1 if direction == 0 else -1
        piece = rings[n].at[slot_of((z - sign * (t - 1)) % 8), pl.ds(a * 64, 64)]
        index = (t - 1) * 2 + a
        send(piece, piece, ring_send_sem.at[n, direction, index], ring_recv_sem.at[n, direction, index], z_peer(sign))

    def ring_step(n, t):
        for a in range(2):
            for direction in range(2):
                if t == 4 and a != direction:
                    continue
                sign = 1 if direction == 0 else -1
                piece = rings[n].at[slot_of((z - sign * t) % 8), pl.ds(a * 64, 64)]
                wait_bytes(piece, ring_recv_sem.at[n, direction, (t - 1) * 2 + a])
                if t + 1 < 4 or (t + 1 == 4 and a == direction):
                    ring_send(n, direction, t + 1, a)

    def ring_start(n):
        @pl.when(foreign == 1)
        def _():
            wait_bytes(rings[n].at[slot], pre_recv.at[n])

        @pl.when(foreign == 0)
        def _():
            wait_bytes(rings[n].at[slot], local_sem.at[2 + n])

        for a in range(2):
            for direction in range(2):
                ring_send(n, direction, 1, a)

    ring_start(0)

    def send_inputs(axis, i, kc):
        for t in range(4):
            pltpu.make_async_remote_copy(
                src_ref=inp.at[:, columns(axis, i, kc, t)],
                dst_ref=xx.at[axis, 2 * i + kc, :, pl.ds(t * 128, 128)],
                send_sem=x_send.at[axis, 2 * i + kc],
                recv_sem=x_recv.at[axis, 2 * i + kc],
                device_id=partner(axis, i, kc),
                device_id_type=MESH,
            ).start()

    for i in ORDER:
        for kc in range(2):
            for axis in range(2):
                send_inputs(axis, i, kc)
    for axis in range(2):
        send_inputs(axis, 0, 1)

    for k in range(1, 8):
        send(mvz.at[z], mvz.at[z], mv_send.at[k - 1], mv_recv.at[k - 1], z_peer(k))

    def transpose_pair(pair, first, second):
        ct[pair, :, 0:128] = jnp.swapaxes(first, 0, 1)
        ct[pair, :, 128:256] = jnp.swapaxes(second, 0, 1)

    def take_cotangent(axis, i):
        ref = cx if axis == 0 else cy
        wait_bytes(ref.at[2 * i], c_recv.at[axis, i, 0])
        send(ref.at[2 * i], ref.at[2 * i + 1], e_send.at[axis, i], c_recv.at[axis, i, 1], partner(0, 0, 1))

    def turn_cotangent(axis, i):
        ref = cx if axis == 0 else cy
        wait_bytes(ref.at[2 * i + 1], c_recv.at[axis, i, 1])
        transpose_pair(axis * 3 + i, ref[2 * i], ref[2 * i + 1])

    def add_inputs(axis, i, first, last):
        if i == 0:
            wait_bytes(xx.at[axis, 0], local_sem.at[4 + axis])
            wait_bytes(xx.at[axis, 1], x_recv.at[axis, 1])
            pair = 0
        else:
            for kc in range(2):
                wait_bytes(xx.at[axis, 2 * i + kc], x_recv.at[axis, 2 * i + kc])
            pair = axis * 3 + i
        cols = pl.ds(axis * 512, 512)

        def body(r, carry):
            rs = pl.ds(pl.multiple_of(r * 256, 256), 256)
            x = xx[axis, 2 * i : 2 * i + 2].reshape(256, 512)
            part = dot(ct[pair, rs, :], x)
            if not first:
                part = part + mf[rs, cols]
            if last:
                mb[rs, cols] = part.astype(BF16)
            else:
                mf[rs, cols] = part
            return carry

        lax.fori_loop(0, 4, body, 0)

    wait_bytes(cx.at[1], c_recv.at[0, 0, 1])
    transpose_pair(0, cx[0], cx[1])
    ring_step(0, 1)
    for i in (1, 3):
        for axis in range(2):
            take_cotangent(axis, i)
    for i in (1, 3):
        for axis in range(2):
            turn_cotangent(axis, i)
    for axis in range(2):
        add_inputs(axis, 0, True, False)
    ring_step(0, 2)
    for axis in range(2):
        take_cotangent(axis, 2)
    for axis in range(2):
        turn_cotangent(axis, 2)
    for i in (1, 3):
        for axis in range(2):
            add_inputs(axis, i, False, False)
        if i == 1:
            ring_step(0, 3)
            ring_start(1)
    for axis in range(2):
        add_inputs(axis, 2, False, True)
    ring_step(0, 4)
    ring_step(1, 1)

    basis = pg[...].reshape(1024, 1024)

    def to_sibling(b, carry):
        rows_b = pl.ds(pl.multiple_of(b * 128 + (1 - c) * 64, 64), 64)
        s0[b] = dot(mb[rows_b, :], basis).astype(BF16)
        return carry

    def own_part(b, carry):
        rows_b = pl.ds(pl.multiple_of(b * 128 + c * 64, 64), 64)
        a_keep[b] = dot(mb[rows_b, :], basis)
        return carry

    for n in range(2):
        lax.fori_loop(n * 4, n * 4 + 4, to_sibling, 0)
        send(s0.at[n * 4 : n * 4 + 4], r0.at[n * 4 : n * 4 + 4], s_send.at[n], s_recv.at[n], partner(0, 0, 1))
    lax.fori_loop(0, 8, own_part, 0)
    for n in range(2):
        wait_bytes(r0.at[n * 4 : n * 4 + 4], s_recv.at[n])

    def add_sibling(b, carry):
        xl_, y_ = b // 4, b % 4
        for hh in range(2):
            rs = slice(hh * 32, hh * 32 + 32)
            total = a_keep[b, rs, :] + r0[b, rs, :].astype(F32)
            a0[hh, xl_, y_] = total[:, 0:512].astype(BF16)
            a1[y_, xl_, hh] = total[:, 512:1024].astype(BF16)
        return carry

    lax.fori_loop(0, 8, add_sibling, 0)

    for i in ORDER:
        hi, lo = PAIRS[i]
        send(a0.at[flip(h, hi), flip(xl, lo)], ra0.at[i - 1], a_send.at[0, i - 1], a_recv.at[0, i - 1], partner(0, i, 0))
        send(a1.at[flip(yh, hi) * 2 + flip(yl, lo)], ra1.at[i - 1], a_send.at[1, i - 1], a_recv.at[1, i - 1], partner(1, i, 0))
    ring_step(1, 2)
    for n, ref in enumerate((ra0, ra1)):
        for i in range(3):
            wait_bytes(ref.at[i], a_recv.at[n, i])
    b0[...] = (a0[h, xl].astype(F32) + ra0[0].astype(F32) + ra0[1].astype(F32) + ra0[2].astype(F32)).astype(BF16)
    b1[...] = (a1[y].astype(F32) + ra1[0].astype(F32) + ra1[1].astype(F32) + ra1[2].astype(F32)).astype(BF16)
    for i in ORDER:
        hi, lo = PAIRS[i]
        send(b0.at[flip(yh, hi) * 2 + flip(yl, lo)], rb0.at[i - 1], b_send.at[0, i - 1], b_recv.at[0, i - 1], partner(1, i, 0))
        send(b1.at[flip(xl, lo), flip(h, hi)], rb1.at[i - 1], b_send.at[1, i - 1], b_recv.at[1, i - 1], partner(0, i, 0))
    for n, ref in enumerate((rb0, rb1)):
        for i in range(3):
            wait_bytes(ref.at[i], b_recv.at[n, i])
    f0 = b0[y].astype(F32) + rb0[0].astype(F32) + rb0[1].astype(F32) + rb0[2].astype(F32)
    f1 = b1[xl, h].astype(F32) + rb1[0].astype(F32) + rb1[1].astype(F32) + rb1[2].astype(F32)
    for zz in range(8):
        cs[zz, 0:4, :] = f0[zz * 4 : zz * 4 + 4]
        cs[zz, 4:8, :] = f1[zz * 4 : zz * 4 + 4]
    for k in range(1, 8):
        send(cs.at[(z + k) % 8], rc.at[k - 1], z_send.at[k - 1], z_recv.at[k - 1], z_peer(k))
    g = cs[z]
    for k in range(1, 8):
        wait_bytes(rc.at[k - 1], z_recv.at[k - 1])
        g = g + rc[k - 1]
    gz[z] = g
    for k in range(1, 8):
        send(gz.at[z], gz.at[z], g_send.at[k - 1], g_recv.at[k - 1], z_peer(k))
    for k in range(1, 8):
        wait_bytes(gz.at[(z - k) % 8], g_recv.at[k - 1])
        wait_bytes(mvz.at[(z - k) % 8], mv_recv.at[k - 1])

    squares = jnp.sum(gz[...] * gz[...])
    ss[0] = jnp.full((8, 128), squares, F32)
    for i in range(4):
        for kc in range(2):
            k = 2 * i + kc
            if k:
                send(ss.at[0], sr_a.at[k - 1], q_send.at[k - 1], q_recv.at[k - 1], partner(0, i, kc))
    total = ss[0]
    for k in range(1, 8):
        wait_bytes(sr_a.at[k - 1], q_recv.at[k - 1])
        total = total + sr_a[k - 1]
    ss[1] = total
    for i in range(1, 4):
        send(ss.at[1], sr_b.at[i - 1], q_send.at[6 + i], q_recv.at[6 + i], partner(1, i, 0))
    for i in range(1, 4):
        wait_bytes(sr_b.at[i - 1], q_recv.at[6 + i])
        total = total + sr_b[i - 1]
    factor = jnp.minimum(1.0, lax.rsqrt(total * (1.0 / ENTRIES) + 1e-06))[0:1, 0:1]

    def adam(gradient, first, second):
        clipped = gradient * factor
        new_first = beta_one * first + (1.0 - beta_one) * clipped
        new_second = beta_two * second + (1.0 - beta_two) * clipped * clipped
        return new_first, new_second

    for zz in range(8):
        first, second = adam(gz[zz], mvz[zz, 0], mvz[zz, 1])
        direction = first / bias_one / (jnp.sqrt(second / bias_two) + 1e-08)
        df[zz * 4 : zz * 4 + 4, 0:512] = direction[0:4]
        df[zz * 4 : zz * 4 + 4, 512:1024] = direction[4:8]
    dall[xl, y, c, h] = df[...].astype(BF16)

    halves = (pl.ds(0, 512), pl.ds(512, 512))
    own = dall.at[xl, y, c, h]
    for i in ORDER:
        for axis in range(2):
            piece = dall.at[xl, y, c, h, :, halves[axis]]
            send(piece, piece, d_send.at[0, axis, i - 1], d_recv.at[0, axis, i - 1], partner(axis, i, 0))

    first, second = adam(gz[z], mvz[z, 0], mvz[z, 1])
    for half in range(2):
        nf[:, half * 512 : half * 512 + 512] = first[half * 4 : half * 4 + 4]
        nv[:, half * 512 : half * 512 + 512] = second[half * 4 : half * 4 + 4]

    for i in ORDER:
        hi, lo = PAIRS[i]
        wait_bytes(dall.at[flip(xl, lo), y, c, flip(h, hi), :, halves[0]], d_recv.at[0, 0, i - 1])
        wait_bytes(dall.at[xl, flip(yh, hi) * 2 + flip(yl, lo), c, h, :, halves[1]], d_recv.at[0, 1, i - 1])
    along_x = lambda y_, c_: dall.at[:, y_, c_, :, :, halves[0]]
    along_y = lambda xl_, h_, c_: dall.at[xl_, :, c_, h_, :, halves[1]]
    for i in ORDER:
        send(along_x(y, c), along_x(y, c), d_send.at[1, 0, i - 1], d_recv.at[1, 0, i - 1], partner(1, i, 0))
        send(along_y(xl, h, c), along_y(xl, h, c), d_send.at[1, 1, i - 1], d_recv.at[1, 1, i - 1], partner(0, i, 0))
    send(along_x(y, c), along_x(y, c), e_send.at[2, 0], e_recv.at[0, 0], partner(0, 0, 1))
    send(along_y(xl, h, c), along_y(xl, h, c), e_send.at[3, 0], e_recv.at[1, 0], partner(0, 0, 1))
    ring_step(1, 3)
    for i in ORDER:
        hi, lo = PAIRS[i]
        y_ = flip(yh, hi) * 2 + flip(yl, lo)
        wait_bytes(along_x(y_, c), d_recv.at[1, 0, i - 1])
        send(along_x(y_, c), along_x(y_, c), e_send.at[2, i], e_recv.at[0, i], partner(0, 0, 1))
        xl_, h_ = flip(xl, lo), flip(h, hi)
        wait_bytes(along_y(xl_, h_, c), d_recv.at[1, 1, i - 1])
        send(along_y(xl_, h_, c), along_y(xl_, h_, c), e_send.at[3, i], e_recv.at[1, i], partner(0, 0, 1))

    ring_step(1, 4)
    for axis in range(2):
        for i in ORDER + (0,):
            ref = cy if axis == 1 and i > 0 else cx
            a = ref[2 * i : 2 * i + 2].reshape(256, 1024)
            b = wg[axis * 4 : axis * 4 + 4].reshape(512, 1024)
            igb[axis, 2 * i : 2 * i + 2] = dot(a, b, NT).astype(BF16).reshape(2, 128, 512)
            for kc in range(2):
                k = 2 * i + kc
                for t in range(4):
                    src = igb.at[axis, k, :, pl.ds(t * 128, 128)]
                    dst = ig.at[:, columns(axis, 0, 0, t)]
                    if k == 0:
                        pltpu.make_async_copy(src, dst, local_sem.at[6 + axis]).start()
                    else:
                        pltpu.make_async_remote_copy(
                            src_ref=src, dst_ref=dst, send_sem=o_send.at[axis, k], recv_sem=o_recv.at[axis, k],
                            device_id=partner(axis, i, kc), device_id_type=MESH,
                        ).start()

    for i in range(4):
        hi, lo = PAIRS[i]
        y_ = flip(yh, hi) * 2 + flip(yl, lo)
        wait_bytes(along_x(y_, 1 - c), e_recv.at[0, i])
        wait_bytes(along_y(flip(xl, lo), flip(h, hi), 1 - c), e_recv.at[1, i])
    own_p.wait()
    for n in range(4):
        xl_, y0 = n // 2, (n % 2) * 2
        rows_d = dall[xl_, y0 : y0 + 2].reshape(256, 1024)
        wu[:, n * 256 : n * 256 + 256] = dot(pblk[...], rows_d, NT).astype(BF16)

    for axis in range(2):
        wait_bytes(igb.at[axis, 0], local_sem.at[6 + axis])
        for k in range(1, 8):
            wait_bytes(xx.at[axis, k], x_send.at[axis, k])
            wait_bytes(igb.at[axis, k], o_send.at[axis, k])
            wait_bytes(igb.at[axis, k], o_recv.at[axis, k])

    @pl.when(odd * (1 - foreign) == 1)
    def _():
        for n in range(2):
            wait_bytes(rings[n].at[slot], pre_send.at[n])

    for copy in sends:
        copy.wait_send()


def local(inputs, cotangent, weight, projector, first_moment_state, second_moment_state):
    anywhere = pl.BlockSpec(memory_space=pl.ANY)
    vmem = pl.BlockSpec(memory_space=pltpu.VMEM)
    dma = pltpu.SemaphoreType.DMA
    V = pltpu.VMEM
    return pl.pallas_call(
        kernel,
        out_shape=(
            jax.ShapeDtypeStruct((TOKENS, WIDTH), BF16),
            jax.ShapeDtypeStruct((512, OUTS), BF16),
            jax.ShapeDtypeStruct((4, RANK), F32),
            jax.ShapeDtypeStruct((4, RANK), F32),
        ),
        in_specs=[anywhere] * 4 + [vmem] * 2,
        out_specs=(anywhere, vmem, vmem, vmem),
        scratch_shapes=[
            V((8, 128, 1024), BF16),
            V((8, 128, 1024), BF16),
            V((7, 1024, 256), BF16),
            V((2, 8, 128, 512), BF16),
            V((8, 128, 1024), BF16),
            V((8, 128, 1024), BF16),
            V((512, 1024), BF16),
            V((1024, 1024), F32),
            V((1024, 1024), BF16),
            V((2, 8, 128, 512), BF16),
            V((8, 64, 1024), BF16),
            V((8, 64, 1024), BF16),
            V((8, 64, 1024), F32),
            V((2, 2, 4, 32, 512), BF16),
            V((4, 2, 2, 32, 512), BF16),
            V((3, 4, 32, 512), BF16),
            V((3, 2, 2, 32, 512), BF16),
            V((4, 32, 512), BF16),
            V((2, 2, 32, 512), BF16),
            V((3, 32, 512), BF16),
            V((3, 32, 512), BF16),
            V((8, 8, 512), F32),
            V((7, 8, 512), F32),
            V((8, 8, 512), F32),
            V((8, 2, 8, 512), F32),
            V((2, 8, 128), F32),
            V((7, 8, 128), F32),
            V((3, 8, 128), F32),
            V((32, 1024), F32),
            V((2, 4, 2, 2, 32, 1024), BF16),
            dma((8,)),
            dma((2, 4)), dma((2, 4, 2)),
            dma((2, 8)), dma((2, 8)),
            dma((2,)), dma((2,)),
            dma((2, 2, 8)), dma((2, 2, 8)),
            dma((7,)), dma((7,)),
            dma((2, 8)), dma((2, 8)),
            dma((2,)), dma((2,)),
            dma((2, 3)), dma((2, 3)),
            dma((2, 3)), dma((2, 3)),
            dma((7,)), dma((7,)),
            dma((7,)), dma((7,)),
            dma((10,)), dma((10,)),
            dma((2, 2, 3)), dma((2, 2, 3)),
            dma((4, 4)), dma((2, 4)),
        ],
        compiler_params=pltpu.CompilerParams(
            collective_id=0, has_side_effects=True, vmem_limit_bytes=56 << 20
        ),
        name="galore",
    )(inputs, cotangent, weight, projector, first_moment_state, second_moment_state)


def solution(mesh):
    return jax.shard_map(
        local,
        mesh=mesh,
        in_specs=(
            P(("dp", "shard"), None),
            P(("dp", "shard"), None),
            P("shard", None),
            P("shard", None),
            P(("dp", "shard"), None),
            P(("dp", "shard"), None),
        ),
        out_specs=(
            P(("dp", "shard"), None),
            P("shard", None),
            P(("dp", "shard"), None),
            P(("dp", "shard"), None),
        ),
        check_vma=False,
    )
```

```python
import jax
import jax.numpy as jnp
from jax import lax
from jax.experimental import pallas as pl
from jax.experimental.pallas import tpu as pltpu
from jax.sharding import PartitionSpec as P

MESH = pl.DeviceIdType.MESH
F32 = jnp.float32
BF16 = jnp.bfloat16

TOKENS = 128
WIDTH = 8192
OUTS = 1024
RANK = 1024
ENTRIES = OUTS * RANK

beta_one = 0.9
beta_two = 0.999
bias_one = 1.0
bias_two = 0.632304575

NN = (((1,), (0,)), ((), ()))
NT = (((1,), (1,)), ((), ()))
TN = (((0,), (0,)), ((), ()))


def dot(a, b, dims=NN):
    return lax.dot_general(a, b, dims, preferred_element_type=F32)


def flip(bit, by):
    return 1 - bit if by else bit


def wait_bytes(ref, sem):
    pltpu.make_async_copy(ref, ref, sem).wait()


PAIRS = ((0, 0), (0, 1), (1, 0), (1, 1))
ORDER = (1, 3, 2)


def kernel(
    inp, cot, w, p, m_in, v_in,
    ig, wu, nf, nv,
    cx, cy, xx, pg, wg, pblk, mf, mb, igb,
    s0, r0, a_keep, a0, a1, ra0, ra1, b0, b1, rb0, rb1, cs, rc, gz, mvz, ss, sr_a, sr_b, df, dall,
    local_sem, c_send, c_recv, x_send, x_recv, pre_send, pre_recv,
    ring_send_sem, ring_recv_sem, mv_send, mv_recv, o_send, o_recv,
    s_send, s_recv, a_send, a_recv, b_send, b_recv, z_send, z_recv, g_send, g_recv,
    q_send, q_recv, d_send, d_recv, e_send, e_recv, f_send, f_recv,
):
    d = lax.axis_index("dp")
    s = lax.axis_index("shard")
    xl = d // 8
    y = (d // 2) % 4
    yh = y // 2
    yl = y % 2
    c = d % 2
    h = s // 8
    z = s % 8

    def device(xl_, yh_, yl_, c_, h_, z_):
        return ((xl_ * 4 + yh_ * 2 + yl_) * 2 + c_, h_ * 8 + z_)

    def partner(axis, i, kc):
        hi, lo = PAIRS[i]
        if axis == 0:
            return device(flip(xl, lo), yh, yl, flip(c, kc), flip(h, hi), z)
        return device(xl, flip(yh, hi), flip(yl, lo), flip(c, kc), h, z)

    def z_peer(k):
        return device(xl, yh, yl, c, h, (z + k) % 8)

    sends = []

    def send(src, dst, ss_, rs_, to):
        copy = pltpu.make_async_remote_copy(
            src_ref=src, dst_ref=dst, send_sem=ss_, recv_sem=rs_, device_id=to, device_id_type=MESH
        )
        copy.start()
        sends.append(copy)

    own_c = pltpu.make_async_copy(cot, cx.at[0], local_sem.at[0])
    own_c.start()
    own_p = pltpu.make_async_copy(p, pblk, local_sem.at[1])
    own_p.start()

    barrier = pltpu.get_barrier_semaphore()
    peers = [partner(0, i, kc) for i in range(4) for kc in range(2) if (i, kc) != (0, 0)]
    peers += [partner(1, i, kc) for i in range(1, 4) for kc in range(2)]
    peers += [z_peer(k) for k in range(1, 8)]
    for peer in peers:
        pl.semaphore_signal(barrier, inc=1, device_id=peer, device_id_type=MESH)

    odd = z % 2
    quarter = (1 - odd) * (xl * 2 + c) + odd * (yl * 2 + c)
    foreign = odd * (h + yh - 2 * h * yh)

    def slot_of(zz):
        return (zz % 2) * 4 + zz // 2

    slot = slot_of(z)

    def half_rows(half):
        return pl.ds(pl.multiple_of(quarter * 128 + half * 64, 64), 64)

    def shared(t):
        e = (odd + t) % 2
        half = (1 - e) * yl + e * xl
        return half, device(xl + e * (1 - 2 * xl), yh, yl + (1 - e) * (1 - 2 * yl), c, h, z)

    @pl.when(foreign == 0)
    def _():
        for n, (src, dst) in enumerate(((p, pg), (w, wg))):
            for half in range(2):
                pltpu.make_async_copy(src.at[half_rows(half)], dst.at[slot, half], local_sem.at[2 + n]).start()

    def columns(axis, i, kc, t):
        hi, lo = PAIRS[i]
        if axis == 0:
            q = flip(xl, lo) * 2 + flip(c, kc)
            block = flip(h, hi) * 8 + 2 * t
        else:
            q = flip(yl, lo) * 2 + flip(c, kc)
            block = flip(yh, hi) * 8 + 2 * t + 1
        return pl.ds(pl.multiple_of(block * 512 + q * 128, 128), 128)

    for axis in range(2):
        for t in range(4):
            pltpu.make_async_copy(
                inp.at[:, columns(axis, 0, 0, t)],
                xx.at[axis, 0, :, pl.ds(t * 128, 128)],
                local_sem.at[4 + axis],
            ).start()

    for n, ref in enumerate((m_in, v_in)):
        for half in range(2):
            mvz[z, n, half * 4 : half * 4 + 4, :] = ref[:, half * 512 : half * 512 + 512]

    pl.semaphore_wait(barrier, len(peers))

    def cross(n, src, dst):
        @pl.when(odd * (1 - foreign) == 1)
        def _():
            for a in range(2) if n == 0 else (1 - xl,):
                pltpu.make_async_remote_copy(
                    src_ref=src.at[half_rows(a)], dst_ref=dst.at[slot, a],
                    send_sem=pre_send.at[n], recv_sem=pre_recv.at[n],
                    device_id=partner(0, 3, 0), device_id_type=MESH,
                ).start()

    cross(0, p, pg)
    rings = (pg, wg)

    def ring_piece(n, direction, t, a):
        piece = rings[n].at[slot_of((z - (1 if direction == 0 else -1) * t) % 8)]
        return piece.at[a] if n == 0 else piece.at[shared(t)[0], pl.ds(a * 32, 32)]

    def ring_copy(n, direction, t, a):
        piece = ring_piece(n, direction, t - 1, a)
        index = (t - 1) * 2 + a
        return pltpu.make_async_remote_copy(
            src_ref=piece, dst_ref=piece,
            send_sem=ring_send_sem.at[n, direction, index], recv_sem=ring_recv_sem.at[n, direction, index],
            device_id=z_peer(1 if direction == 0 else -1), device_id_type=MESH,
        )

    def neighbour_half(direction, t, other):
        half = shared(t)[0]
        return wg.at[slot_of((z - (1 if direction == 0 else -1) * t) % 8), 1 - half if other else half]

    def hand_over(direction, t, index):
        piece = neighbour_half(direction, t, False)
        send(piece, piece, f_send.at[index], f_recv.at[index], shared(t)[1])

    def ring_step(n, t):
        for a in range(2):
            for direction in range(2):
                if t == 4 and a != direction:
                    continue
                wait_bytes(ring_piece(n, direction, t, a), ring_recv_sem.at[n, direction, (t - 1) * 2 + a])
                if t + 1 < 4 or (t + 1 == 4 and a == direction):
                    onward = ring_copy(n, direction, t + 1, a)
                    onward.start()
                    sends.append(onward)
        for direction in range((2 if t < 4 else 1) if n == 1 else 0):
            hand_over(direction, t, (t - 1) * 2 + direction)

    def ring_start(n, which):
        @pl.when(foreign == which)
        def _():
            if which:
                wait_bytes(rings[n].at[slot] if n == 0 else rings[n].at[slot, xl], pre_recv.at[n])
                if n == 1:
                    own_half().start()
            else:
                wait_bytes(rings[n].at[slot], local_sem.at[2 + n])
            for a in range(2):
                for direction in range(2):
                    ring_copy(n, direction, 1, a).start()

        if which:
            sends.extend(ring_copy(n, direction, 1, a) for a in range(2) for direction in range(2))

    def own_half():
        piece = wg.at[slot, xl]
        return pltpu.make_async_remote_copy(
            src_ref=piece, dst_ref=piece, send_sem=f_send.at[7], recv_sem=f_recv.at[7],
            device_id=partner(0, 1, 0), device_id_type=MESH,
        )

    def ring_end():
        for t in range(1, 5):
            for direction in range(2 if t < 4 else 1):
                wait_bytes(neighbour_half(direction, t, True), f_recv.at[(t - 1) * 2 + direction])

        @pl.when(foreign == 1)
        def _():
            wait_bytes(wg.at[slot, 1 - xl], f_recv.at[7])
            wait_bytes(wg.at[slot, xl], f_send.at[7])

    ring_start(0, 0)

    def send_inputs(axis, i, kc):
        for t in range(4):
            pltpu.make_async_remote_copy(
                src_ref=inp.at[:, columns(axis, i, kc, t)],
                dst_ref=xx.at[axis, 2 * i + kc, :, pl.ds(t * 128, 128)],
                send_sem=x_send.at[axis, 2 * i + kc],
                recv_sem=x_recv.at[axis, 2 * i + kc],
                device_id=partner(axis, i, kc),
                device_id_type=MESH,
            ).start()

    own_c.wait()
    send(cx.at[0], cx.at[1], c_send.at[0, 0], c_recv.at[0, 0, 1], partner(0, 0, 1))
    for axis in (1, 0):
        if axis == 0:
            @pl.when(odd * (1 - foreign) == 1)
            def _():
                wait_bytes(pg.at[slot], pre_send.at[0])

        for i in ORDER:
            dst = (cx if axis == 0 else cy).at[2 * i]
            send(cx.at[0], dst, c_send.at[axis, i], c_recv.at[axis, i, 0], partner(axis, i, 0))
        for i in ORDER:
            for kc in range(2):
                send_inputs(axis, i, kc)
        send_inputs(axis, 0, 1)

    ring_start(0, 1)
    cross(1, w, wg)

    def take_cotangent(axis, i):
        ref = cx if axis == 0 else cy
        wait_bytes(ref.at[2 * i], c_recv.at[axis, i, 0])
        send(ref.at[2 * i], ref.at[2 * i + 1], e_send.at[axis, i], c_recv.at[axis, i, 1], partner(0, 0, 1))

    def pair_of(axis, i):
        return (cy if axis == 1 and i > 0 else cx), slice(2 * i, 2 * i + 2)

    def add_inputs(axis, i, first, last):
        ref, pair = pair_of(axis, i)
        if i == 0:
            wait_bytes(xx.at[axis, 0], local_sem.at[4 + axis])
            wait_bytes(xx.at[axis, 1], x_recv.at[axis, 1])
        else:
            wait_bytes(ref.at[2 * i + 1], c_recv.at[axis, i, 1])
            for kc in range(2):
                wait_bytes(xx.at[axis, 2 * i + kc], x_recv.at[axis, 2 * i + kc])
        cols = slice(axis * 512, axis * 512 + 512)
        x = xx[axis, pair].reshape(256, 512)
        for r in range(4):
            rs = slice(r * 256, r * 256 + 256)
            part = dot(ref[pair, :, rs].reshape(256, 256), x, TN)
            if not first:
                part = part + mf[rs, cols]
            if last:
                part = part.astype(BF16).reshape(2, 2, 64, 512)
                for core in range(2):
                    mb[core, 2 * r : 2 * r + 2, :, cols] = part[:, core]
            else:
                mf[rs, cols] = part

    ring_step(0, 1)
    ring_step(0, 2)
    for axis in (1, 0):
        for i in (1, 3):
            take_cotangent(axis, i)
    ring_step(0, 3)
    ring_start(1, 0)
    ring_start(1, 1)
    ring_step(0, 4)
    for axis in (1, 0):
        take_cotangent(axis, 2)
    wait_bytes(cx.at[1], c_recv.at[0, 0, 1])
    for axis in (1, 0):
        add_inputs(axis, 0, True, False)
    ring_step(1, 1)
    for i in (1, 3, 2):
        for axis in (1, 0):
            add_inputs(axis, i, False, i == 2)

    returns = [(axis, i) for i in ORDER + (0,) for axis in range(2)]

    def return_gradient(first, last):
        for axis, i in returns[first:last]:
            ref, pair = pair_of(axis, i)
            a = ref[pair].reshape(256, 1024)
            b = wg[axis * 4 : axis * 4 + 4].reshape(512, 1024)
            igb[axis, pair] = dot(a, b, NT).astype(BF16).reshape(2, 128, 512)
            for kc in range(2):
                k = 2 * i + kc
                for t in range(4):
                    src = igb.at[axis, k, :, pl.ds(t * 128, 128)]
                    dst = ig.at[:, columns(axis, 0, 0, t)]
                    if k == 0:
                        pltpu.make_async_copy(src, dst, local_sem.at[6 + axis]).start()
                    else:
                        pltpu.make_async_remote_copy(
                            src_ref=src, dst_ref=dst, send_sem=o_send.at[axis, k], recv_sem=o_recv.at[axis, k],
                            device_id=partner(axis, i, kc), device_id_type=MESH,
                        ).start()

    basis = pg[...].reshape(1024, 1024)

    for n in range(2):
        group = slice(n * 4, n * 4 + 4)
        s0[group] = dot(mb[1 - c, group].reshape(256, 1024), basis).astype(BF16).reshape(4, 64, 1024)
        send(s0.at[group], r0.at[group], s_send.at[n], s_recv.at[n], partner(0, 0, 1))
    ring_step(1, 2)
    for n in range(2):
        group = slice(n * 4, n * 4 + 4)
        a_keep[group] = dot(mb[c, group].reshape(256, 1024), basis).reshape(4, 64, 1024)
    ring_step(1, 3)
    for n in range(2):
        wait_bytes(r0.at[n * 4 : n * 4 + 4], s_recv.at[n])

    for b in range(8):
        xl_, y_ = b // 4, b % 4
        total = a_keep[b] + r0[b].astype(F32)
        for hh in range(2):
            rs = slice(hh * 32, hh * 32 + 32)
            a0[hh, xl_, y_] = total[rs, 0:512].astype(BF16)
            a1[y_, xl_, hh] = total[rs, 512:1024].astype(BF16)

    for i in ORDER:
        hi, lo = PAIRS[i]
        send(a0.at[flip(h, hi), flip(xl, lo)], ra0.at[i - 1], a_send.at[0, i - 1], a_recv.at[0, i - 1], partner(0, i, 0))
        send(a1.at[flip(yh, hi) * 2 + flip(yl, lo)], ra1.at[i - 1], a_send.at[1, i - 1], a_recv.at[1, i - 1], partner(1, i, 0))
    ring_step(1, 4)
    for k in range(1, 8):
        send(mvz.at[z], mvz.at[z], mv_send.at[k - 1], mv_recv.at[k - 1], z_peer(k))
    for n, ref in enumerate((ra0, ra1)):
        for i in range(3):
            wait_bytes(ref.at[i], a_recv.at[n, i])
    b0[...] = (a0[h, xl].astype(F32) + ra0[0].astype(F32) + ra0[1].astype(F32) + ra0[2].astype(F32)).astype(BF16)
    b1[...] = (a1[y].astype(F32) + ra1[0].astype(F32) + ra1[1].astype(F32) + ra1[2].astype(F32)).astype(BF16)
    for i in ORDER:
        hi, lo = PAIRS[i]
        send(b0.at[flip(yh, hi) * 2 + flip(yl, lo)], rb0.at[i - 1], b_send.at[0, i - 1], b_recv.at[0, i - 1], partner(1, i, 0))
        send(b1.at[flip(xl, lo), flip(h, hi)], rb1.at[i - 1], b_send.at[1, i - 1], b_recv.at[1, i - 1], partner(0, i, 0))
    for n, ref in enumerate((rb0, rb1)):
        for i in range(3):
            wait_bytes(ref.at[i], b_recv.at[n, i])
    f0 = b0[y].astype(F32) + rb0[0].astype(F32) + rb0[1].astype(F32) + rb0[2].astype(F32)
    f1 = b1[xl, h].astype(F32) + rb1[0].astype(F32) + rb1[1].astype(F32) + rb1[2].astype(F32)
    for zz in range(8):
        cs[zz, 0:4, :] = f0[zz * 4 : zz * 4 + 4]
        cs[zz, 4:8, :] = f1[zz * 4 : zz * 4 + 4]
    for k in range(1, 8):
        send(cs.at[(z + k) % 8], rc.at[k - 1], z_send.at[k - 1], z_recv.at[k - 1], z_peer(k))
    ring_end()
    return_gradient(0, 3)
    g = cs[z]
    for k in range(1, 8):
        wait_bytes(rc.at[k - 1], z_recv.at[k - 1])
        g = g + rc[k - 1]
    gz[z] = g
    for k in range(1, 8):
        send(gz.at[z], gz.at[z], g_send.at[k - 1], g_recv.at[k - 1], z_peer(k))
    return_gradient(3, 6)
    for k in range(1, 8):
        wait_bytes(gz.at[(z - k) % 8], g_recv.at[k - 1])
        wait_bytes(mvz.at[(z - k) % 8], mv_recv.at[k - 1])

    squares = jnp.sum(gz[...] * gz[...])
    ss[0] = jnp.full((8, 128), squares, F32)
    for i in range(4):
        for kc in range(2):
            k = 2 * i + kc
            if k:
                send(ss.at[0], sr_a.at[k - 1], q_send.at[k - 1], q_recv.at[k - 1], partner(0, i, kc))
    return_gradient(6, 8)
    total = ss[0]
    for k in range(1, 8):
        wait_bytes(sr_a.at[k - 1], q_recv.at[k - 1])
        total = total + sr_a[k - 1]
    ss[1] = total
    for i in range(1, 4):
        send(ss.at[1], sr_b.at[i - 1], q_send.at[6 + i], q_recv.at[6 + i], partner(1, i, 0))
    for i in range(1, 4):
        wait_bytes(sr_b.at[i - 1], q_recv.at[6 + i])
        total = total + sr_b[i - 1]
    factor = jnp.minimum(1.0, lax.rsqrt(total * (1.0 / ENTRIES) + 1e-06))[0:1, 0:1]

    def adam(gradient, first, second):
        clipped = gradient * factor
        new_first = beta_one * first + (1.0 - beta_one) * clipped
        new_second = beta_two * second + (1.0 - beta_two) * clipped * clipped
        return new_first, new_second

    for zz in range(8):
        first, second = adam(gz[zz], mvz[zz, 0], mvz[zz, 1])
        direction = first / bias_one / (jnp.sqrt(second / bias_two) + 1e-08)
        df[zz * 4 : zz * 4 + 4, 0:512] = direction[0:4]
        df[zz * 4 : zz * 4 + 4, 512:1024] = direction[4:8]
    dall[xl, y, c, h] = df[...].astype(BF16)

    halves = (pl.ds(0, 512), pl.ds(512, 512))
    own = dall.at[xl, y, c, h]
    for i in ORDER:
        for axis in range(2):
            piece = dall.at[xl, y, c, h, :, halves[axis]]
            send(piece, piece, d_send.at[0, axis, i - 1], d_recv.at[0, axis, i - 1], partner(axis, i, 0))

    first, second = adam(gz[z], mvz[z, 0], mvz[z, 1])
    for half in range(2):
        nf[:, half * 512 : half * 512 + 512] = first[half * 4 : half * 4 + 4]
        nv[:, half * 512 : half * 512 + 512] = second[half * 4 : half * 4 + 4]

    for i in ORDER:
        hi, lo = PAIRS[i]
        wait_bytes(dall.at[flip(xl, lo), y, c, flip(h, hi), :, halves[0]], d_recv.at[0, 0, i - 1])
        wait_bytes(dall.at[xl, flip(yh, hi) * 2 + flip(yl, lo), c, h, :, halves[1]], d_recv.at[0, 1, i - 1])
    along_x = lambda y_, c_: dall.at[:, y_, c_, :, :, halves[0]]
    along_y = lambda xl_, h_, c_: dall.at[xl_, :, c_, h_, :, halves[1]]
    for i in ORDER:
        send(along_x(y, c), along_x(y, c), d_send.at[1, 0, i - 1], d_recv.at[1, 0, i - 1], partner(1, i, 0))
        send(along_y(xl, h, c), along_y(xl, h, c), d_send.at[1, 1, i - 1], d_recv.at[1, 1, i - 1], partner(0, i, 0))
    send(along_x(y, c), along_x(y, c), e_send.at[2, 0], e_recv.at[0, 0], partner(0, 0, 1))
    send(along_y(xl, h, c), along_y(xl, h, c), e_send.at[3, 0], e_recv.at[1, 0], partner(0, 0, 1))
    for i in ORDER:
        hi, lo = PAIRS[i]
        y_ = flip(yh, hi) * 2 + flip(yl, lo)
        wait_bytes(along_x(y_, c), d_recv.at[1, 0, i - 1])
        send(along_x(y_, c), along_x(y_, c), e_send.at[2, i], e_recv.at[0, i], partner(0, 0, 1))
        xl_, h_ = flip(xl, lo), flip(h, hi)
        wait_bytes(along_y(xl_, h_, c), d_recv.at[1, 1, i - 1])
        send(along_y(xl_, h_, c), along_y(xl_, h_, c), e_send.at[3, i], e_recv.at[1, i], partner(0, 0, 1))

    for i in range(4):
        hi, lo = PAIRS[i]
        y_ = flip(yh, hi) * 2 + flip(yl, lo)
        wait_bytes(along_x(y_, 1 - c), e_recv.at[0, i])
        wait_bytes(along_y(flip(xl, lo), flip(h, hi), 1 - c), e_recv.at[1, i])
    own_p.wait()
    for n in range(4):
        xl_, y0 = n // 2, (n % 2) * 2
        rows_d = dall[xl_, y0 : y0 + 2].reshape(256, 1024)
        wu[:, n * 256 : n * 256 + 256] = dot(pblk[...], rows_d, NT).astype(BF16)

    for axis in range(2):
        wait_bytes(igb.at[axis, 0], local_sem.at[6 + axis])
        for k in range(1, 8):
            wait_bytes(xx.at[axis, k], x_send.at[axis, k])
            wait_bytes(igb.at[axis, k], o_send.at[axis, k])
            wait_bytes(igb.at[axis, k], o_recv.at[axis, k])

    @pl.when(odd * (1 - foreign) == 1)
    def _():
        wait_bytes(wg.at[slot, 0], pre_send.at[1])

    for copy in sends:
        copy.wait_send()


def local(inputs, cotangent, weight, projector, first_moment_state, second_moment_state):
    anywhere = pl.BlockSpec(memory_space=pl.ANY)
    vmem = pl.BlockSpec(memory_space=pltpu.VMEM)
    dma = pltpu.SemaphoreType.DMA
    V = pltpu.VMEM
    return pl.pallas_call(
        kernel,
        out_shape=(
            jax.ShapeDtypeStruct((TOKENS, WIDTH), BF16),
            jax.ShapeDtypeStruct((512, OUTS), BF16),
            jax.ShapeDtypeStruct((4, RANK), F32),
            jax.ShapeDtypeStruct((4, RANK), F32),
        ),
        in_specs=[anywhere] * 4 + [vmem] * 2,
        out_specs=(anywhere, vmem, vmem, vmem),
        scratch_shapes=[
            V((8, 128, 1024), BF16),
            V((8, 128, 1024), BF16),
            V((2, 8, 128, 512), BF16),
            V((8, 2, 64, 1024), BF16),
            V((8, 2, 64, 1024), BF16),
            V((512, 1024), BF16),
            V((1024, 1024), F32),
            V((2, 8, 64, 1024), BF16),
            V((2, 8, 128, 512), BF16),
            V((8, 64, 1024), BF16),
            V((8, 64, 1024), BF16),
            V((8, 64, 1024), F32),
            V((2, 2, 4, 32, 512), BF16),
            V((4, 2, 2, 32, 512), BF16),
            V((3, 4, 32, 512), BF16),
            V((3, 2, 2, 32, 512), BF16),
            V((4, 32, 512), BF16),
            V((2, 2, 32, 512), BF16),
            V((3, 32, 512), BF16),
            V((3, 32, 512), BF16),
            V((8, 8, 512), F32),
            V((7, 8, 512), F32),
            V((8, 8, 512), F32),
            V((8, 2, 8, 512), F32),
            V((2, 8, 128), F32),
            V((7, 8, 128), F32),
            V((3, 8, 128), F32),
            V((32, 1024), F32),
            V((2, 4, 2, 2, 32, 1024), BF16),
            dma((8,)),
            dma((2, 4)), dma((2, 4, 2)),
            dma((2, 8)), dma((2, 8)),
            dma((2,)), dma((2,)),
            dma((2, 2, 8)), dma((2, 2, 8)),
            dma((7,)), dma((7,)),
            dma((2, 8)), dma((2, 8)),
            dma((2,)), dma((2,)),
            dma((2, 3)), dma((2, 3)),
            dma((2, 3)), dma((2, 3)),
            dma((7,)), dma((7,)),
            dma((7,)), dma((7,)),
            dma((10,)), dma((10,)),
            dma((2, 2, 3)), dma((2, 2, 3)),
            dma((4, 4)), dma((2, 4)),
            dma((8,)), dma((8,)),
        ],
        compiler_params=pltpu.CompilerParams(
            collective_id=0, has_side_effects=True, vmem_limit_bytes=56 << 20
        ),
        name="galore",
    )(inputs, cotangent, weight, projector, first_moment_state, second_moment_state)


def solution(mesh):
    return jax.shard_map(
        local,
        mesh=mesh,
        in_specs=(
            P(("dp", "shard"), None),
            P(("dp", "shard"), None),
            P("shard", None),
            P("shard", None),
            P(("dp", "shard"), None),
            P(("dp", "shard"), None),
        ),
        out_specs=(
            P(("dp", "shard"), None),
            P("shard", None),
            P(("dp", "shard"), None),
            P(("dp", "shard"), None),
        ),
        check_vma=False,
    )
```

```python
import jax
import jax.numpy as jnp
from jax import lax
from jax.experimental import pallas as pl
from jax.experimental.pallas import tpu as pltpu
from jax.sharding import PartitionSpec as P

MESH = pl.DeviceIdType.MESH
F32 = jnp.float32
BF16 = jnp.bfloat16

TOKENS = 128
WIDTH = 8192
OUTS = 1024
RANK = 1024
ENTRIES = OUTS * RANK

beta_one = 0.9
beta_two = 0.999
bias_one = 1.0
bias_two = 0.632304575

NN = (((1,), (0,)), ((), ()))
NT = (((1,), (1,)), ((), ()))
TN = (((0,), (0,)), ((), ()))


def dot(a, b, dims=NN):
    return lax.dot_general(a, b, dims, preferred_element_type=F32)


def flip(bit, by):
    return 1 - bit if by else bit


def wait_bytes(ref, sem):
    pltpu.make_async_copy(ref, ref, sem).wait()


PAIRS = ((0, 0), (0, 1), (1, 0), (1, 1))
ORDER = (1, 3, 2)


def kernel(
    inp, cot, w, p, m_in, v_in,
    ig, wu, nf, nv,
    cx, cy, xx, pg, wg, pblk, mf, mb, igb,
    s0, r0, a_keep, a0, a1, ra0, ra1, b0, b1, rb0, rb1, cs, rc, gz, mvz, ss, sr_a, sr_b, df, dall,
    local_sem, c_send, c_recv, x_send, x_recv, pre_send, pre_recv,
    ring_send_sem, ring_recv_sem, mv_send, mv_recv, o_send, o_recv,
    s_send, s_recv, a_send, a_recv, b_send, b_recv, z_send, z_recv, g_send, g_recv,
    q_send, q_recv, d_send, d_recv, e_send, e_recv, f_send, f_recv,
):
    d = lax.axis_index("dp")
    s = lax.axis_index("shard")
    xl = d // 8
    y = (d // 2) % 4
    yh = y // 2
    yl = y % 2
    c = d % 2
    h = s // 8
    z = s % 8

    def device(xl_, yh_, yl_, c_, h_, z_):
        return ((xl_ * 4 + yh_ * 2 + yl_) * 2 + c_, h_ * 8 + z_)

    def partner(axis, i, kc):
        hi, lo = PAIRS[i]
        if axis == 0:
            return device(flip(xl, lo), yh, yl, flip(c, kc), flip(h, hi), z)
        return device(xl, flip(yh, hi), flip(yl, lo), flip(c, kc), h, z)

    def z_peer(k):
        return device(xl, yh, yl, c, h, (z + k) % 8)

    sends = []

    def send(src, dst, ss_, rs_, to):
        copy = pltpu.make_async_remote_copy(
            src_ref=src, dst_ref=dst, send_sem=ss_, recv_sem=rs_, device_id=to, device_id_type=MESH
        )
        copy.start()
        sends.append(copy)

    own_c = pltpu.make_async_copy(cot, cx.at[0], local_sem.at[0])
    own_c.start()
    own_p = pltpu.make_async_copy(p, pblk, local_sem.at[1])
    own_p.start()

    barrier = pltpu.get_barrier_semaphore()
    peers = [partner(0, i, kc) for i in range(4) for kc in range(2) if (i, kc) != (0, 0)]
    peers += [partner(1, i, kc) for i in range(1, 4) for kc in range(2)]
    peers += [z_peer(k) for k in range(1, 8)]
    for peer in peers:
        pl.semaphore_signal(barrier, inc=1, device_id=peer, device_id_type=MESH)

    odd = z % 2
    quarter = (1 - odd) * (xl * 2 + c) + odd * (yl * 2 + c)
    foreign = odd * (h + yh - 2 * h * yh)

    def slot_of(zz):
        return (zz % 2) * 4 + zz // 2

    slot = slot_of(z)

    def half_rows(half):
        return pl.ds(pl.multiple_of(quarter * 128 + half * 64, 64), 64)

    def shared(t):
        e = (odd + t) % 2
        half = (1 - e) * yl + e * xl
        return half, device(xl + e * (1 - 2 * xl), yh, yl + (1 - e) * (1 - 2 * yl), c, h, z)

    @pl.when(foreign == 0)
    def _():
        for n, (src, dst) in enumerate(((p, pg), (w, wg))):
            for half in range(2):
                pltpu.make_async_copy(src.at[half_rows(half)], dst.at[slot, half], local_sem.at[2 + n]).start()

    def columns(axis, i, kc, t):
        hi, lo = PAIRS[i]
        if axis == 0:
            q = flip(xl, lo) * 2 + flip(c, kc)
            block = flip(h, hi) * 8 + 2 * t
        else:
            q = flip(yl, lo) * 2 + flip(c, kc)
            block = flip(yh, hi) * 8 + 2 * t + 1
        return pl.ds(pl.multiple_of(block * 512 + q * 128, 128), 128)

    for axis in range(2):
        for t in range(4):
            pltpu.make_async_copy(
                inp.at[:, columns(axis, 0, 0, t)],
                xx.at[axis, 0, :, pl.ds(t * 128, 128)],
                local_sem.at[4 + axis],
            ).start()

    for n, ref in enumerate((m_in, v_in)):
        for half in range(2):
            mvz[z, n, half * 4 : half * 4 + 4, :] = ref[:, half * 512 : half * 512 + 512]

    pl.semaphore_wait(barrier, len(peers))

    def cross(n, src, dst):
        @pl.when(odd * (1 - foreign) == 1)
        def _():
            for a in range(2) if n == 0 else (1 - xl,):
                pltpu.make_async_remote_copy(
                    src_ref=src.at[half_rows(a)], dst_ref=dst.at[slot, a],
                    send_sem=pre_send.at[n], recv_sem=pre_recv.at[n],
                    device_id=partner(0, 3, 0), device_id_type=MESH,
                ).start()

    cross(0, p, pg)
    rings = (pg, wg)

    def ring_piece(n, direction, t, a):
        piece = rings[n].at[slot_of((z - (1 if direction == 0 else -1) * t) % 8)]
        return piece.at[a] if n == 0 else piece.at[shared(t)[0], pl.ds(a * 32, 32)]

    def ring_copy(n, direction, t, a):
        piece = ring_piece(n, direction, t - 1, a)
        index = (t - 1) * 2 + a
        return pltpu.make_async_remote_copy(
            src_ref=piece, dst_ref=piece,
            send_sem=ring_send_sem.at[n, direction, index], recv_sem=ring_recv_sem.at[n, direction, index],
            device_id=z_peer(1 if direction == 0 else -1), device_id_type=MESH,
        )

    def neighbour_half(direction, t, other):
        half = shared(t)[0]
        return wg.at[slot_of((z - (1 if direction == 0 else -1) * t) % 8), 1 - half if other else half]

    def hand_over(direction, t, index):
        piece = neighbour_half(direction, t, False)
        send(piece, piece, f_send.at[index], f_recv.at[index], shared(t)[1])

    def ring_step(n, t):
        for a in range(2):
            for direction in range(2):
                if t == 4 and a != direction:
                    continue
                wait_bytes(ring_piece(n, direction, t, a), ring_recv_sem.at[n, direction, (t - 1) * 2 + a])
                if t + 1 < 4 or (t + 1 == 4 and a == direction):
                    onward = ring_copy(n, direction, t + 1, a)
                    onward.start()
                    sends.append(onward)
        for direction in range((2 if t < 4 else 1) if n == 1 else 0):
            hand_over(direction, t, (t - 1) * 2 + direction)

    def ring_start(n, which):
        @pl.when(foreign == which)
        def _():
            if which:
                wait_bytes(rings[n].at[slot] if n == 0 else rings[n].at[slot, xl], pre_recv.at[n])
                if n == 1:
                    own_half().start()
            else:
                wait_bytes(rings[n].at[slot], local_sem.at[2 + n])
            for a in range(2):
                for direction in range(2):
                    ring_copy(n, direction, 1, a).start()

        if which:
            sends.extend(ring_copy(n, direction, 1, a) for a in range(2) for direction in range(2))

    def own_half():
        piece = wg.at[slot, xl]
        return pltpu.make_async_remote_copy(
            src_ref=piece, dst_ref=piece, send_sem=f_send.at[7], recv_sem=f_recv.at[7],
            device_id=partner(0, 1, 0), device_id_type=MESH,
        )

    def ring_end():
        for t in range(1, 5):
            for direction in range(2 if t < 4 else 1):
                wait_bytes(neighbour_half(direction, t, True), f_recv.at[(t - 1) * 2 + direction])

        @pl.when(foreign == 1)
        def _():
            wait_bytes(wg.at[slot, 1 - xl], f_recv.at[7])
            wait_bytes(wg.at[slot, xl], f_send.at[7])

    ring_start(0, 0)

    def send_inputs(axis, i, kc):
        for t in range(4):
            pltpu.make_async_remote_copy(
                src_ref=inp.at[:, columns(axis, i, kc, t)],
                dst_ref=xx.at[axis, 2 * i + kc, :, pl.ds(t * 128, 128)],
                send_sem=x_send.at[axis, 2 * i + kc],
                recv_sem=x_recv.at[axis, 2 * i + kc],
                device_id=partner(axis, i, kc),
                device_id_type=MESH,
            ).start()

    own_c.wait()
    send(cx.at[0], cx.at[1], c_send.at[0, 0], c_recv.at[0, 0, 1], partner(0, 0, 1))
    for axis in (1, 0):
        if axis == 0:
            @pl.when(odd * (1 - foreign) == 1)
            def _():
                wait_bytes(pg.at[slot], pre_send.at[0])

        for i in ORDER:
            dst = (cx if axis == 0 else cy).at[2 * i]
            send(cx.at[0], dst, c_send.at[axis, i], c_recv.at[axis, i, 0], partner(axis, i, 0))
        for i in ORDER:
            for kc in range(2):
                send_inputs(axis, i, kc)
        send_inputs(axis, 0, 1)

    ring_start(0, 1)
    cross(1, w, wg)

    def take_cotangent(axis, i):
        ref = cx if axis == 0 else cy
        wait_bytes(ref.at[2 * i], c_recv.at[axis, i, 0])
        send(ref.at[2 * i], ref.at[2 * i + 1], e_send.at[axis, i], c_recv.at[axis, i, 1], partner(0, 0, 1))

    def pair_of(axis, i):
        return (cy if axis == 1 and i > 0 else cx), slice(2 * i, 2 * i + 2)

    def add_inputs(axis, i, first, last):
        ref, pair = pair_of(axis, i)
        if i == 0:
            wait_bytes(xx.at[axis, 0], local_sem.at[4 + axis])
            wait_bytes(xx.at[axis, 1], x_recv.at[axis, 1])
        else:
            wait_bytes(ref.at[2 * i + 1], c_recv.at[axis, i, 1])
            for kc in range(2):
                wait_bytes(xx.at[axis, 2 * i + kc], x_recv.at[axis, 2 * i + kc])
        cols = slice(axis * 512, axis * 512 + 512)
        x = xx[axis, pair].reshape(256, 512)
        for r in range(4):
            rs = slice(r * 256, r * 256 + 256)
            part = dot(ref[pair, :, rs].reshape(256, 256), x, TN)
            if not first:
                part = part + mf[rs, cols]
            if last:
                part = part.astype(BF16).reshape(2, 2, 64, 512)
                for core in range(2):
                    mb[core, 2 * r : 2 * r + 2, :, cols] = part[:, core]
            else:
                mf[rs, cols] = part

    ring_step(0, 1)
    ring_step(0, 2)
    for axis in (1, 0):
        for i in (1, 3):
            take_cotangent(axis, i)
    ring_step(0, 3)
    ring_start(1, 0)
    ring_start(1, 1)
    ring_step(0, 4)
    for axis in (1, 0):
        take_cotangent(axis, 2)
    wait_bytes(cx.at[1], c_recv.at[0, 0, 1])
    for axis in (1, 0):
        add_inputs(axis, 0, True, False)
    for i in (1, 3, 2):
        for axis in (1, 0):
            add_inputs(axis, i, False, i == 2)

    returns = [(axis, i) for i in ORDER + (0,) for axis in range(2)]

    def return_gradient(first, last):
        for axis, i in returns[first:last]:
            ref, pair = pair_of(axis, i)
            a = ref[pair].reshape(256, 1024)
            b = wg[axis * 4 : axis * 4 + 4].reshape(512, 1024)
            igb[axis, pair] = dot(a, b, NT).astype(BF16).reshape(2, 128, 512)
            for kc in range(2):
                k = 2 * i + kc
                for t in range(4):
                    src = igb.at[axis, k, :, pl.ds(t * 128, 128)]
                    dst = ig.at[:, columns(axis, 0, 0, t)]
                    if k == 0:
                        pltpu.make_async_copy(src, dst, local_sem.at[6 + axis]).start()
                    else:
                        pltpu.make_async_remote_copy(
                            src_ref=src, dst_ref=dst, send_sem=o_send.at[axis, k], recv_sem=o_recv.at[axis, k],
                            device_id=partner(axis, i, kc), device_id_type=MESH,
                        ).start()

    halves = (pl.ds(0, 512), pl.ds(512, 512))

    def product(core, half):
        return dot(mb[core].reshape(512, 1024), pg[:, :, :, halves[half]].reshape(1024, 512)).reshape(8, 64, 512)

    for half in range(2):
        s0[half] = product(1 - c, half).astype(BF16)
        send(s0.at[half], r0.at[half], s_send.at[half], s_recv.at[half], partner(0, 0, 1))
    ring_step(1, 1)
    for half in range(2):
        a_keep[...] = product(c, half)
        wait_bytes(r0.at[half], s_recv.at[half])
        for b in range(8):
            total = (a_keep[b] + r0[half, b].astype(F32)).astype(BF16)
            for hh in range(2):
                if half == 0:
                    a0[hh, b // 4, b % 4] = total[hh * 32 : hh * 32 + 32]
                else:
                    a1[b % 4, b // 4, hh] = total[hh * 32 : hh * 32 + 32]
        for i in ORDER:
            hi, lo = PAIRS[i]
            if half == 0:
                src, dst = a0.at[flip(h, hi), flip(xl, lo)], ra0
            else:
                src, dst = a1.at[flip(yh, hi) * 2 + flip(yl, lo)], ra1
            send(src, dst.at[i - 1], a_send.at[half, i - 1], a_recv.at[half, i - 1], partner(half, i, 0))
    ring_step(1, 2)
    for k in range(1, 8):
        send(mvz.at[z], mvz.at[z], mv_send.at[k - 1], mv_recv.at[k - 1], z_peer(k))
    for n, ref in enumerate((ra0, ra1)):
        for i in range(3):
            wait_bytes(ref.at[i], a_recv.at[n, i])
    b0[...] = (a0[h, xl].astype(F32) + ra0[0].astype(F32) + ra0[1].astype(F32) + ra0[2].astype(F32)).astype(BF16)
    b1[...] = (a1[y].astype(F32) + ra1[0].astype(F32) + ra1[1].astype(F32) + ra1[2].astype(F32)).astype(BF16)
    for i in ORDER:
        hi, lo = PAIRS[i]
        send(b0.at[flip(yh, hi) * 2 + flip(yl, lo)], rb0.at[i - 1], b_send.at[0, i - 1], b_recv.at[0, i - 1], partner(1, i, 0))
        send(b1.at[flip(xl, lo), flip(h, hi)], rb1.at[i - 1], b_send.at[1, i - 1], b_recv.at[1, i - 1], partner(0, i, 0))
    ring_step(1, 3)
    for n, ref in enumerate((rb0, rb1)):
        for i in range(3):
            wait_bytes(ref.at[i], b_recv.at[n, i])
    f0 = b0[y].astype(F32) + rb0[0].astype(F32) + rb0[1].astype(F32) + rb0[2].astype(F32)
    f1 = b1[xl, h].astype(F32) + rb1[0].astype(F32) + rb1[1].astype(F32) + rb1[2].astype(F32)
    for zz in range(8):
        cs[zz, 0:4, :] = f0[zz * 4 : zz * 4 + 4]
        cs[zz, 4:8, :] = f1[zz * 4 : zz * 4 + 4]
    for k in range(1, 8):
        send(cs.at[(z + k) % 8], rc.at[k - 1], z_send.at[k - 1], z_recv.at[k - 1], z_peer(k))
    ring_step(1, 4)
    g = cs[z]
    for k in range(1, 8):
        wait_bytes(rc.at[k - 1], z_recv.at[k - 1])
        g = g + rc[k - 1]
    gz[z] = g
    for k in range(1, 8):
        send(gz.at[z], gz.at[z], g_send.at[k - 1], g_recv.at[k - 1], z_peer(k))
    ring_end()
    return_gradient(0, 4)
    for k in range(1, 8):
        wait_bytes(gz.at[(z - k) % 8], g_recv.at[k - 1])
        wait_bytes(mvz.at[(z - k) % 8], mv_recv.at[k - 1])

    squares = jnp.sum(gz[...] * gz[...])
    ss[0] = jnp.full((8, 128), squares, F32)
    for i in range(4):
        for kc in range(2):
            k = 2 * i + kc
            if k:
                send(ss.at[0], sr_a.at[k - 1], q_send.at[k - 1], q_recv.at[k - 1], partner(0, i, kc))
    return_gradient(4, 8)
    total = ss[0]
    for k in range(1, 8):
        wait_bytes(sr_a.at[k - 1], q_recv.at[k - 1])
        total = total + sr_a[k - 1]
    ss[1] = total
    for i in range(1, 4):
        send(ss.at[1], sr_b.at[i - 1], q_send.at[6 + i], q_recv.at[6 + i], partner(1, i, 0))
    for i in range(1, 4):
        wait_bytes(sr_b.at[i - 1], q_recv.at[6 + i])
        total = total + sr_b[i - 1]
    factor = jnp.minimum(1.0, lax.rsqrt(total * (1.0 / ENTRIES) + 1e-06))[0:1, 0:1]

    def adam(gradient, first, second):
        clipped = gradient * factor
        new_first = beta_one * first + (1.0 - beta_one) * clipped
        new_second = beta_two * second + (1.0 - beta_two) * clipped * clipped
        return new_first, new_second

    for zz in range(8):
        first, second = adam(gz[zz], mvz[zz, 0], mvz[zz, 1])
        direction = first / bias_one / (jnp.sqrt(second / bias_two) + 1e-08)
        df[zz * 4 : zz * 4 + 4, 0:512] = direction[0:4]
        df[zz * 4 : zz * 4 + 4, 512:1024] = direction[4:8]
    dall[xl, y, c, h] = df[...].astype(BF16)

    for i in ORDER:
        for axis in range(2):
            piece = dall.at[xl, y, c, h, :, halves[axis]]
            send(piece, piece, d_send.at[0, axis, i - 1], d_recv.at[0, axis, i - 1], partner(axis, i, 0))

    first, second = adam(gz[z], mvz[z, 0], mvz[z, 1])
    for half in range(2):
        nf[:, half * 512 : half * 512 + 512] = first[half * 4 : half * 4 + 4]
        nv[:, half * 512 : half * 512 + 512] = second[half * 4 : half * 4 + 4]

    for i in ORDER:
        hi, lo = PAIRS[i]
        wait_bytes(dall.at[flip(xl, lo), y, c, flip(h, hi), :, halves[0]], d_recv.at[0, 0, i - 1])
        wait_bytes(dall.at[xl, flip(yh, hi) * 2 + flip(yl, lo), c, h, :, halves[1]], d_recv.at[0, 1, i - 1])
    along_x = lambda y_, c_: dall.at[:, y_, c_, :, :, halves[0]]
    along_y = lambda xl_, h_, c_: dall.at[xl_, :, c_, h_, :, halves[1]]
    for i in ORDER:
        send(along_x(y, c), along_x(y, c), d_send.at[1, 0, i - 1], d_recv.at[1, 0, i - 1], partner(1, i, 0))
        send(along_y(xl, h, c), along_y(xl, h, c), d_send.at[1, 1, i - 1], d_recv.at[1, 1, i - 1], partner(0, i, 0))
    send(along_x(y, c), along_x(y, c), e_send.at[2, 0], e_recv.at[0, 0], partner(0, 0, 1))
    send(along_y(xl, h, c), along_y(xl, h, c), e_send.at[3, 0], e_recv.at[1, 0], partner(0, 0, 1))
    for i in ORDER:
        hi, lo = PAIRS[i]
        y_ = flip(yh, hi) * 2 + flip(yl, lo)
        wait_bytes(along_x(y_, c), d_recv.at[1, 0, i - 1])
        send(along_x(y_, c), along_x(y_, c), e_send.at[2, i], e_recv.at[0, i], partner(0, 0, 1))
        xl_, h_ = flip(xl, lo), flip(h, hi)
        wait_bytes(along_y(xl_, h_, c), d_recv.at[1, 1, i - 1])
        send(along_y(xl_, h_, c), along_y(xl_, h_, c), e_send.at[3, i], e_recv.at[1, i], partner(0, 0, 1))

    for i in range(4):
        hi, lo = PAIRS[i]
        y_ = flip(yh, hi) * 2 + flip(yl, lo)
        wait_bytes(along_x(y_, 1 - c), e_recv.at[0, i])
        wait_bytes(along_y(flip(xl, lo), flip(h, hi), 1 - c), e_recv.at[1, i])
    own_p.wait()
    for n in range(4):
        xl_, y0 = n // 2, (n % 2) * 2
        rows_d = dall[xl_, y0 : y0 + 2].reshape(256, 1024)
        wu[:, n * 256 : n * 256 + 256] = dot(pblk[...], rows_d, NT).astype(BF16)

    for axis in range(2):
        wait_bytes(igb.at[axis, 0], local_sem.at[6 + axis])
        for k in range(1, 8):
            wait_bytes(xx.at[axis, k], x_send.at[axis, k])
            wait_bytes(igb.at[axis, k], o_send.at[axis, k])
            wait_bytes(igb.at[axis, k], o_recv.at[axis, k])

    @pl.when(odd * (1 - foreign) == 1)
    def _():
        wait_bytes(wg.at[slot, 0], pre_send.at[1])

    for copy in sends:
        copy.wait_send()


def local(inputs, cotangent, weight, projector, first_moment_state, second_moment_state):
    anywhere = pl.BlockSpec(memory_space=pl.ANY)
    vmem = pl.BlockSpec(memory_space=pltpu.VMEM)
    dma = pltpu.SemaphoreType.DMA
    V = pltpu.VMEM
    return pl.pallas_call(
        kernel,
        out_shape=(
            jax.ShapeDtypeStruct((TOKENS, WIDTH), BF16),
            jax.ShapeDtypeStruct((512, OUTS), BF16),
            jax.ShapeDtypeStruct((4, RANK), F32),
            jax.ShapeDtypeStruct((4, RANK), F32),
        ),
        in_specs=[anywhere] * 4 + [vmem] * 2,
        out_specs=(anywhere, vmem, vmem, vmem),
        scratch_shapes=[
            V((8, 128, 1024), BF16),
            V((8, 128, 1024), BF16),
            V((2, 8, 128, 512), BF16),
            V((8, 2, 64, 1024), BF16),
            V((8, 2, 64, 1024), BF16),
            V((512, 1024), BF16),
            V((1024, 1024), F32),
            V((2, 8, 64, 1024), BF16),
            V((2, 8, 128, 512), BF16),
            V((2, 8, 64, 512), BF16),
            V((2, 8, 64, 512), BF16),
            V((8, 64, 512), F32),
            V((2, 2, 4, 32, 512), BF16),
            V((4, 2, 2, 32, 512), BF16),
            V((3, 4, 32, 512), BF16),
            V((3, 2, 2, 32, 512), BF16),
            V((4, 32, 512), BF16),
            V((2, 2, 32, 512), BF16),
            V((3, 32, 512), BF16),
            V((3, 32, 512), BF16),
            V((8, 8, 512), F32),
            V((7, 8, 512), F32),
            V((8, 8, 512), F32),
            V((8, 2, 8, 512), F32),
            V((2, 8, 128), F32),
            V((7, 8, 128), F32),
            V((3, 8, 128), F32),
            V((32, 1024), F32),
            V((2, 4, 2, 2, 32, 1024), BF16),
            dma((8,)),
            dma((2, 4)), dma((2, 4, 2)),
            dma((2, 8)), dma((2, 8)),
            dma((2,)), dma((2,)),
            dma((2, 2, 8)), dma((2, 2, 8)),
            dma((7,)), dma((7,)),
            dma((2, 8)), dma((2, 8)),
            dma((2,)), dma((2,)),
            dma((2, 3)), dma((2, 3)),
            dma((2, 3)), dma((2, 3)),
            dma((7,)), dma((7,)),
            dma((7,)), dma((7,)),
            dma((10,)), dma((10,)),
            dma((2, 2, 3)), dma((2, 2, 3)),
            dma((4, 4)), dma((2, 4)),
            dma((8,)), dma((8,)),
        ],
        compiler_params=pltpu.CompilerParams(
            collective_id=0, has_side_effects=True, vmem_limit_bytes=56 << 20
        ),
        name="galore",
    )(inputs, cotangent, weight, projector, first_moment_state, second_moment_state)


def solution(mesh):
    return jax.shard_map(
        local,
        mesh=mesh,
        in_specs=(
            P(("dp", "shard"), None),
            P(("dp", "shard"), None),
            P("shard", None),
            P("shard", None),
            P(("dp", "shard"), None),
            P(("dp", "shard"), None),
        ),
        out_specs=(
            P(("dp", "shard"), None),
            P("shard", None),
            P(("dp", "shard"), None),
            P(("dp", "shard"), None),
        ),
        check_vma=False,
    )
```

```python
import jax
import jax.numpy as jnp
from jax import lax
from jax.experimental import pallas as pl
from jax.experimental.pallas import tpu as pltpu
from jax.sharding import PartitionSpec as P

MESH = pl.DeviceIdType.MESH
F32 = jnp.float32
BF16 = jnp.bfloat16

TOKENS = 128
WIDTH = 8192
OUTS = 1024
RANK = 1024
ENTRIES = OUTS * RANK

beta_one = 0.9
beta_two = 0.999
bias_one = 1.0
bias_two = 0.632304575

NN = (((1,), (0,)), ((), ()))
NT = (((1,), (1,)), ((), ()))
TN = (((0,), (0,)), ((), ()))


def dot(a, b, dims=NN):
    return lax.dot_general(a, b, dims, preferred_element_type=F32)


def flip(bit, by):
    return 1 - bit if by else bit


def wait_bytes(ref, sem):
    pltpu.make_async_copy(ref, ref, sem).wait()


PAIRS = ((0, 0), (0, 1), (1, 0), (1, 1))
ORDER = (1, 3, 2)


def kernel(
    inp, cot, w, p, m_in, v_in,
    ig, wu, nf, nv,
    cx, cy, xx, pg, wg, pblk, mf, mb, igb,
    s0, r0, a_keep, a0, a1, ra0, ra1, b0, b1, rb0, rb1, cs, rc, gz, mvz, ss, sr_a, sr_b, df, dall,
    local_sem, c_send, c_recv, x_send, x_recv, pre_send, pre_recv,
    ring_send_sem, ring_recv_sem, mv_send, mv_recv, o_send, o_recv,
    s_send, s_recv, a_send, a_recv, b_send, b_recv, z_send, z_recv, g_send, g_recv,
    q_send, q_recv, d_send, d_recv, e_send, e_recv, f_send, f_recv,
):
    d = lax.axis_index("dp")
    s = lax.axis_index("shard")
    xl = d // 8
    y = (d // 2) % 4
    yh = y // 2
    yl = y % 2
    c = d % 2
    h = s // 8
    z = s % 8

    def device(xl_, yh_, yl_, c_, h_, z_):
        return ((xl_ * 4 + yh_ * 2 + yl_) * 2 + c_, h_ * 8 + z_)

    def partner(axis, i, kc):
        hi, lo = PAIRS[i]
        if axis == 0:
            return device(flip(xl, lo), yh, yl, flip(c, kc), flip(h, hi), z)
        return device(xl, flip(yh, hi), flip(yl, lo), flip(c, kc), h, z)

    def z_peer(k):
        return device(xl, yh, yl, c, h, (z + k) % 8)

    sends = []

    def send(src, dst, ss_, rs_, to):
        copy = pltpu.make_async_remote_copy(
            src_ref=src, dst_ref=dst, send_sem=ss_, recv_sem=rs_, device_id=to, device_id_type=MESH
        )
        copy.start()
        sends.append(copy)

    own_c = pltpu.make_async_copy(cot, cx.at[0], local_sem.at[0])
    own_c.start()
    own_p = pltpu.make_async_copy(p, pblk, local_sem.at[1])
    own_p.start()

    barrier = pltpu.get_barrier_semaphore()
    peers = [partner(0, i, kc) for i in range(4) for kc in range(2) if (i, kc) != (0, 0)]
    peers += [partner(1, i, kc) for i in range(1, 4) for kc in range(2)]
    peers += [z_peer(k) for k in (1, 7)]
    for peer in peers:
        pl.semaphore_signal(barrier, inc=1, device_id=peer, device_id_type=MESH)

    odd = z % 2
    quarter = (1 - odd) * (xl * 2 + c) + odd * (yl * 2 + c)
    foreign = odd * (h + yh - 2 * h * yh)

    def slot_of(zz):
        return (zz % 2) * 4 + zz // 2

    slot = slot_of(z)

    def half_rows(half):
        return pl.ds(pl.multiple_of(quarter * 128 + half * 64, 64), 64)

    def shared(t):
        e = (odd + t) % 2
        half = (1 - e) * yl + e * xl
        return half, device(xl + e * (1 - 2 * xl), yh, yl + (1 - e) * (1 - 2 * yl), c, h, z)

    @pl.when(foreign == 0)
    def _():
        for n, (src, dst) in enumerate(((p, pg), (w, wg))):
            for half in range(2):
                pltpu.make_async_copy(src.at[half_rows(half)], dst.at[slot, half], local_sem.at[2 + n]).start()

    def columns(axis, i, kc, t):
        hi, lo = PAIRS[i]
        if axis == 0:
            q = flip(xl, lo) * 2 + flip(c, kc)
            block = flip(h, hi) * 8 + 2 * t
        else:
            q = flip(yl, lo) * 2 + flip(c, kc)
            block = flip(yh, hi) * 8 + 2 * t + 1
        return pl.ds(pl.multiple_of(block * 512 + q * 128, 128), 128)

    for axis in range(2):
        for t in range(4):
            pltpu.make_async_copy(
                inp.at[:, columns(axis, 0, 0, t)],
                xx.at[axis, 0, :, pl.ds(t * 128, 128)],
                local_sem.at[4 + axis],
            ).start()

    for n, ref in enumerate((m_in, v_in)):
        for half in range(2):
            mvz[z, n, half * 4 : half * 4 + 4, :] = ref[:, half * 512 : half * 512 + 512]

    pl.semaphore_wait(barrier, len(peers))

    def cross(n, src, dst):
        @pl.when(odd * (1 - foreign) == 1)
        def _():
            for a in range(2) if n == 0 else (1 - xl,):
                pltpu.make_async_remote_copy(
                    src_ref=src.at[half_rows(a)], dst_ref=dst.at[slot, a],
                    send_sem=pre_send.at[n], recv_sem=pre_recv.at[n],
                    device_id=partner(0, 3, 0), device_id_type=MESH,
                ).start()

    cross(0, p, pg)
    rings = (pg, wg)

    def ring_piece(n, direction, t, a):
        piece = rings[n].at[slot_of((z - (1 if direction == 0 else -1) * t) % 8)]
        return piece.at[a] if n == 0 else piece.at[shared(t)[0], pl.ds(a * 32, 32)]

    def ring_copy(n, direction, t, a):
        piece = ring_piece(n, direction, t - 1, a)
        index = (t - 1) * 2 + a
        return pltpu.make_async_remote_copy(
            src_ref=piece, dst_ref=piece,
            send_sem=ring_send_sem.at[n, direction, index], recv_sem=ring_recv_sem.at[n, direction, index],
            device_id=z_peer(1 if direction == 0 else -1), device_id_type=MESH,
        )

    def neighbour_half(direction, t, other):
        half = shared(t)[0]
        return wg.at[slot_of((z - (1 if direction == 0 else -1) * t) % 8), 1 - half if other else half]

    def hand_over(direction, t, index):
        piece = neighbour_half(direction, t, False)
        send(piece, piece, f_send.at[index], f_recv.at[index], shared(t)[1])

    def ring_step(n, t):
        for a in range(2):
            for direction in range(2):
                if t == 4 and a != direction:
                    continue
                wait_bytes(ring_piece(n, direction, t, a), ring_recv_sem.at[n, direction, (t - 1) * 2 + a])
                if t + 1 < 4 or (t + 1 == 4 and a == direction):
                    onward = ring_copy(n, direction, t + 1, a)
                    onward.start()
                    sends.append(onward)
        for direction in range((2 if t < 4 else 1) if n == 1 else 0):
            hand_over(direction, t, (t - 1) * 2 + direction)

    def ring_start(n, which):
        @pl.when(foreign == which)
        def _():
            if which:
                wait_bytes(rings[n].at[slot] if n == 0 else rings[n].at[slot, xl], pre_recv.at[n])
                if n == 1:
                    own_half().start()
            else:
                wait_bytes(rings[n].at[slot], local_sem.at[2 + n])
            for a in range(2):
                for direction in range(2):
                    ring_copy(n, direction, 1, a).start()

        if which:
            sends.extend(ring_copy(n, direction, 1, a) for a in range(2) for direction in range(2))

    def own_half():
        piece = wg.at[slot, xl]
        return pltpu.make_async_remote_copy(
            src_ref=piece, dst_ref=piece, send_sem=f_send.at[7], recv_sem=f_recv.at[7],
            device_id=partner(0, 1, 0), device_id_type=MESH,
        )

    def ring_end():
        for t in range(1, 5):
            for direction in range(2 if t < 4 else 1):
                wait_bytes(neighbour_half(direction, t, True), f_recv.at[(t - 1) * 2 + direction])

        @pl.when(foreign == 1)
        def _():
            wait_bytes(wg.at[slot, 1 - xl], f_recv.at[7])
            wait_bytes(wg.at[slot, xl], f_send.at[7])

    ring_start(0, 0)

    def send_inputs(axis, i, kc):
        for t in range(4):
            pltpu.make_async_remote_copy(
                src_ref=inp.at[:, columns(axis, i, kc, t)],
                dst_ref=xx.at[axis, 2 * i + kc, :, pl.ds(t * 128, 128)],
                send_sem=x_send.at[axis, 2 * i + kc],
                recv_sem=x_recv.at[axis, 2 * i + kc],
                device_id=partner(axis, i, kc),
                device_id_type=MESH,
            ).start()

    own_c.wait()
    send(cx.at[0], cx.at[1], c_send.at[0, 0], c_recv.at[0, 0, 1], partner(0, 0, 1))
    for axis in (1, 0):
        if axis == 0:
            @pl.when(odd * (1 - foreign) == 1)
            def _():
                wait_bytes(pg.at[slot], pre_send.at[0])

        for i in ORDER:
            dst = (cx if axis == 0 else cy).at[2 * i]
            send(cx.at[0], dst, c_send.at[axis, i], c_recv.at[axis, i, 0], partner(axis, i, 0))
        for i in ORDER:
            for kc in range(2):
                send_inputs(axis, i, kc)
        send_inputs(axis, 0, 1)

    ring_start(0, 1)
    cross(1, w, wg)

    def take_cotangent(axis, i):
        ref = cx if axis == 0 else cy
        wait_bytes(ref.at[2 * i], c_recv.at[axis, i, 0])
        send(ref.at[2 * i], ref.at[2 * i + 1], e_send.at[axis, i], c_recv.at[axis, i, 1], partner(0, 0, 1))

    def pair_of(axis, i):
        return (cy if axis == 1 and i > 0 else cx), slice(2 * i, 2 * i + 2)

    def add_inputs(axis, i, first, last):
        ref, pair = pair_of(axis, i)
        if i == 0:
            wait_bytes(xx.at[axis, 0], local_sem.at[4 + axis])
            wait_bytes(xx.at[axis, 1], x_recv.at[axis, 1])
        else:
            wait_bytes(ref.at[2 * i + 1], c_recv.at[axis, i, 1])
            for kc in range(2):
                wait_bytes(xx.at[axis, 2 * i + kc], x_recv.at[axis, 2 * i + kc])
        cols = slice(axis * 512, axis * 512 + 512)
        x = xx[axis, pair].reshape(256, 512)
        for r in range(4):
            rs = slice(r * 256, r * 256 + 256)
            part = dot(ref[pair, :, rs].reshape(256, 256), x, TN)
            if not first:
                part = part + mf[rs, cols]
            if last:
                part = part.astype(BF16).reshape(2, 2, 64, 512)
                for core in range(2):
                    mb[core, 2 * r : 2 * r + 2, :, cols] = part[:, core]
            else:
                mf[rs, cols] = part

    ring_step(0, 1)
    ring_step(0, 2)
    for axis in (1, 0):
        for i in (1, 3):
            take_cotangent(axis, i)
    ring_step(0, 3)
    ring_start(1, 0)
    ring_start(1, 1)
    ring_step(0, 4)
    for axis in (1, 0):
        take_cotangent(axis, 2)
    wait_bytes(cx.at[1], c_recv.at[0, 0, 1])
    for axis in (1, 0):
        add_inputs(axis, 0, True, False)
    for i in (1, 3, 2):
        for axis in (1, 0):
            add_inputs(axis, i, False, i == 2)

    returns = [(axis, i) for i in ORDER + (0,) for axis in range(2)]

    def return_gradient(first, last):
        for axis, i in returns[first:last]:
            ref, pair = pair_of(axis, i)
            a = ref[pair].reshape(256, 1024)
            b = wg[axis * 4 : axis * 4 + 4].reshape(512, 1024)
            igb[axis, pair] = dot(a, b, NT).astype(BF16).reshape(2, 128, 512)
            for kc in range(2):
                k = 2 * i + kc
                for t in range(4):
                    src = igb.at[axis, k, :, pl.ds(t * 128, 128)]
                    dst = ig.at[:, columns(axis, 0, 0, t)]
                    if k == 0:
                        pltpu.make_async_copy(src, dst, local_sem.at[6 + axis]).start()
                    else:
                        pltpu.make_async_remote_copy(
                            src_ref=src, dst_ref=dst, send_sem=o_send.at[axis, k], recv_sem=o_recv.at[axis, k],
                            device_id=partner(axis, i, kc), device_id_type=MESH,
                        ).start()

    halves = (pl.ds(0, 512), pl.ds(512, 512))

    def product(core, half):
        return dot(mb[core].reshape(512, 1024), pg[:, :, :, halves[half]].reshape(1024, 512)).reshape(8, 64, 512)

    for half in range(2):
        s0[half] = product(1 - c, half).astype(BF16)
        send(s0.at[half], r0.at[half], s_send.at[half], s_recv.at[half], partner(0, 0, 1))
    ring_step(1, 1)
    for half in range(2):
        a_keep[...] = product(c, half)
        wait_bytes(r0.at[half], s_recv.at[half])
        for b in range(8):
            total = (a_keep[b] + r0[half, b].astype(F32)).astype(BF16)
            for hh in range(2):
                if half == 0:
                    a0[hh, b // 4, b % 4] = total[hh * 32 : hh * 32 + 32]
                else:
                    a1[b % 4, b // 4, hh] = total[hh * 32 : hh * 32 + 32]
        for i in ORDER:
            hi, lo = PAIRS[i]
            if half == 0:
                src, dst = a0.at[flip(h, hi), flip(xl, lo)], ra0
            else:
                src, dst = a1.at[flip(yh, hi) * 2 + flip(yl, lo)], ra1
            send(src, dst.at[i - 1], a_send.at[half, i - 1], a_recv.at[half, i - 1], partner(half, i, 0))
    ring_step(1, 2)
    for k in range(1, 8):
        send(mvz.at[z], mvz.at[z], mv_send.at[k - 1], mv_recv.at[k - 1], z_peer(k))
    for n, ref in enumerate((ra0, ra1)):
        for i in range(3):
            wait_bytes(ref.at[i], a_recv.at[n, i])
    b0[...] = (a0[h, xl].astype(F32) + ra0[0].astype(F32) + ra0[1].astype(F32) + ra0[2].astype(F32)).astype(BF16)
    b1[...] = (a1[y].astype(F32) + ra1[0].astype(F32) + ra1[1].astype(F32) + ra1[2].astype(F32)).astype(BF16)
    for i in ORDER:
        hi, lo = PAIRS[i]
        send(b0.at[flip(yh, hi) * 2 + flip(yl, lo)], rb0.at[i - 1], b_send.at[0, i - 1], b_recv.at[0, i - 1], partner(1, i, 0))
        send(b1.at[flip(xl, lo), flip(h, hi)], rb1.at[i - 1], b_send.at[1, i - 1], b_recv.at[1, i - 1], partner(0, i, 0))
    ring_step(1, 3)
    for n, ref in enumerate((rb0, rb1)):
        for i in range(3):
            wait_bytes(ref.at[i], b_recv.at[n, i])
    f0 = b0[y].astype(F32) + rb0[0].astype(F32) + rb0[1].astype(F32) + rb0[2].astype(F32)
    f1 = b1[xl, h].astype(F32) + rb1[0].astype(F32) + rb1[1].astype(F32) + rb1[2].astype(F32)
    for zz in range(8):
        cs[zz, 0:4, :] = f0[zz * 4 : zz * 4 + 4]
        cs[zz, 4:8, :] = f1[zz * 4 : zz * 4 + 4]
    for k in range(1, 8):
        send(cs.at[(z + k) % 8], rc.at[k - 1], z_send.at[k - 1], z_recv.at[k - 1], z_peer(k))
    ring_step(1, 4)
    g = cs[z]
    for k in range(1, 8):
        wait_bytes(rc.at[k - 1], z_recv.at[k - 1])
        g = g + rc[k - 1]
    gz[z] = g
    for k in range(1, 8):
        send(gz.at[z], gz.at[z], g_send.at[k - 1], g_recv.at[k - 1], z_peer(k))
    ring_end()
    return_gradient(0, 4)
    for k in range(1, 8):
        wait_bytes(gz.at[(z - k) % 8], g_recv.at[k - 1])
        wait_bytes(mvz.at[(z - k) % 8], mv_recv.at[k - 1])

    squares = jnp.sum(gz[...] * gz[...])
    ss[0] = jnp.full((8, 128), squares, F32)
    for i in range(4):
        for kc in range(2):
            k = 2 * i + kc
            if k:
                send(ss.at[0], sr_a.at[k - 1], q_send.at[k - 1], q_recv.at[k - 1], partner(0, i, kc))
    return_gradient(4, 8)
    total = ss[0]
    for k in range(1, 8):
        wait_bytes(sr_a.at[k - 1], q_recv.at[k - 1])
        total = total + sr_a[k - 1]
    ss[1] = total
    for i in range(1, 4):
        send(ss.at[1], sr_b.at[i - 1], q_send.at[6 + i], q_recv.at[6 + i], partner(1, i, 0))
    for i in range(1, 4):
        wait_bytes(sr_b.at[i - 1], q_recv.at[6 + i])
        total = total + sr_b[i - 1]
    factor = jnp.minimum(1.0, lax.rsqrt(total * (1.0 / ENTRIES) + 1e-06))[0:1, 0:1]

    def adam(gradient, first, second):
        clipped = gradient * factor
        new_first = beta_one * first + (1.0 - beta_one) * clipped
        new_second = beta_two * second + (1.0 - beta_two) * clipped * clipped
        return new_first, new_second

    for zz in range(8):
        first, second = adam(gz[zz], mvz[zz, 0], mvz[zz, 1])
        direction = first / bias_one / (jnp.sqrt(second / bias_two) + 1e-08)
        df[zz * 4 : zz * 4 + 4, 0:512] = direction[0:4]
        df[zz * 4 : zz * 4 + 4, 512:1024] = direction[4:8]
    dall[xl, y, c, h] = df[...].astype(BF16)

    for i in ORDER:
        for axis in range(2):
            piece = dall.at[xl, y, c, h, :, halves[axis]]
            send(piece, piece, d_send.at[0, axis, i - 1], d_recv.at[0, axis, i - 1], partner(axis, i, 0))

    first, second = adam(gz[z], mvz[z, 0], mvz[z, 1])
    for half in range(2):
        nf[:, half * 512 : half * 512 + 512] = first[half * 4 : half * 4 + 4]
        nv[:, half * 512 : half * 512 + 512] = second[half * 4 : half * 4 + 4]

    for i in ORDER:
        hi, lo = PAIRS[i]
        wait_bytes(dall.at[flip(xl, lo), y, c, flip(h, hi), :, halves[0]], d_recv.at[0, 0, i - 1])
        wait_bytes(dall.at[xl, flip(yh, hi) * 2 + flip(yl, lo), c, h, :, halves[1]], d_recv.at[0, 1, i - 1])
    along_x = lambda y_, c_: dall.at[:, y_, c_, :, :, halves[0]]
    along_y = lambda xl_, h_, c_: dall.at[xl_, :, c_, h_, :, halves[1]]
    for i in ORDER:
        send(along_x(y, c), along_x(y, c), d_send.at[1, 0, i - 1], d_recv.at[1, 0, i - 1], partner(1, i, 0))
        send(along_y(xl, h, c), along_y(xl, h, c), d_send.at[1, 1, i - 1], d_recv.at[1, 1, i - 1], partner(0, i, 0))
    send(along_x(y, c), along_x(y, c), e_send.at[2, 0], e_recv.at[0, 0], partner(0, 0, 1))
    send(along_y(xl, h, c), along_y(xl, h, c), e_send.at[3, 0], e_recv.at[1, 0], partner(0, 0, 1))
    for i in ORDER:
        hi, lo = PAIRS[i]
        y_ = flip(yh, hi) * 2 + flip(yl, lo)
        wait_bytes(along_x(y_, c), d_recv.at[1, 0, i - 1])
        send(along_x(y_, c), along_x(y_, c), e_send.at[2, i], e_recv.at[0, i], partner(0, 0, 1))
        xl_, h_ = flip(xl, lo), flip(h, hi)
        wait_bytes(along_y(xl_, h_, c), d_recv.at[1, 1, i - 1])
        send(along_y(xl_, h_, c), along_y(xl_, h_, c), e_send.at[3, i], e_recv.at[1, i], partner(0, 0, 1))

    for i in range(4):
        hi, lo = PAIRS[i]
        y_ = flip(yh, hi) * 2 + flip(yl, lo)
        wait_bytes(along_x(y_, 1 - c), e_recv.at[0, i])
        wait_bytes(along_y(flip(xl, lo), flip(h, hi), 1 - c), e_recv.at[1, i])
    own_p.wait()
    for n in range(4):
        xl_, y0 = n // 2, (n % 2) * 2
        rows_d = dall[xl_, y0 : y0 + 2].reshape(256, 1024)
        wu[:, n * 256 : n * 256 + 256] = dot(pblk[...], rows_d, NT).astype(BF16)

    for axis in range(2):
        wait_bytes(igb.at[axis, 0], local_sem.at[6 + axis])
        for k in range(1, 8):
            wait_bytes(xx.at[axis, k], x_send.at[axis, k])
            wait_bytes(igb.at[axis, k], o_send.at[axis, k])
            wait_bytes(igb.at[axis, k], o_recv.at[axis, k])

    @pl.when(odd * (1 - foreign) == 1)
    def _():
        wait_bytes(wg.at[slot, 0], pre_send.at[1])

    for copy in sends:
        copy.wait_send()


def local(inputs, cotangent, weight, projector, first_moment_state, second_moment_state):
    anywhere = pl.BlockSpec(memory_space=pl.ANY)
    vmem = pl.BlockSpec(memory_space=pltpu.VMEM)
    dma = pltpu.SemaphoreType.DMA
    V = pltpu.VMEM
    return pl.pallas_call(
        kernel,
        out_shape=(
            jax.ShapeDtypeStruct((TOKENS, WIDTH), BF16),
            jax.ShapeDtypeStruct((512, OUTS), BF16),
            jax.ShapeDtypeStruct((4, RANK), F32),
            jax.ShapeDtypeStruct((4, RANK), F32),
        ),
        in_specs=[anywhere] * 4 + [vmem] * 2,
        out_specs=(anywhere, vmem, vmem, vmem),
        scratch_shapes=[
            V((8, 128, 1024), BF16),
            V((8, 128, 1024), BF16),
            V((2, 8, 128, 512), BF16),
            V((8, 2, 64, 1024), BF16),
            V((8, 2, 64, 1024), BF16),
            V((512, 1024), BF16),
            V((1024, 1024), F32),
            V((2, 8, 64, 1024), BF16),
            V((2, 8, 128, 512), BF16),
            V((2, 8, 64, 512), BF16),
            V((2, 8, 64, 512), BF16),
            V((8, 64, 512), F32),
            V((2, 2, 4, 32, 512), BF16),
            V((4, 2, 2, 32, 512), BF16),
            V((3, 4, 32, 512), BF16),
            V((3, 2, 2, 32, 512), BF16),
            V((4, 32, 512), BF16),
            V((2, 2, 32, 512), BF16),
            V((3, 32, 512), BF16),
            V((3, 32, 512), BF16),
            V((8, 8, 512), F32),
            V((7, 8, 512), F32),
            V((8, 8, 512), F32),
            V((8, 2, 8, 512), F32),
            V((2, 8, 128), F32),
            V((7, 8, 128), F32),
            V((3, 8, 128), F32),
            V((32, 1024), F32),
            V((2, 4, 2, 2, 32, 1024), BF16),
            dma((8,)),
            dma((2, 4)), dma((2, 4, 2)),
            dma((2, 8)), dma((2, 8)),
            dma((2,)), dma((2,)),
            dma((2, 2, 8)), dma((2, 2, 8)),
            dma((7,)), dma((7,)),
            dma((2, 8)), dma((2, 8)),
            dma((2,)), dma((2,)),
            dma((2, 3)), dma((2, 3)),
            dma((2, 3)), dma((2, 3)),
            dma((7,)), dma((7,)),
            dma((7,)), dma((7,)),
            dma((10,)), dma((10,)),
            dma((2, 2, 3)), dma((2, 2, 3)),
            dma((4, 4)), dma((2, 4)),
            dma((8,)), dma((8,)),
        ],
        compiler_params=pltpu.CompilerParams(
            collective_id=0, has_side_effects=True, vmem_limit_bytes=56 << 20
        ),
        name="galore",
    )(inputs, cotangent, weight, projector, first_moment_state, second_moment_state)


def solution(mesh):
    return jax.shard_map(
        local,
        mesh=mesh,
        in_specs=(
            P(("dp", "shard"), None),
            P(("dp", "shard"), None),
            P("shard", None),
            P("shard", None),
            P(("dp", "shard"), None),
            P(("dp", "shard"), None),
        ),
        out_specs=(
            P(("dp", "shard"), None),
            P("shard", None),
            P(("dp", "shard"), None),
            P(("dp", "shard"), None),
        ),
        check_vma=False,
    )
```
